256 devices in a mesh: gx: 16 (over y, x), gy: 8 (over z), gz: 2 (over core).
Axes of the slice: x: 4, y: 4, z: 8, core: 2. Of those that a mesh axis runs over, the one named last changes fastest.
Arguments:
- electric_x: float32 [512, 128, 1024], P('gx', 'gy', 'gz'), may hold values from -32 to 32
- electric_z: float32 [512, 128, 1024], P('gx', 'gy', 'gz'), may hold values from -32 to 32
- magnetic_x: float32 [512, 128, 1024], P('gx', 'gy', 'gz'), may hold values from -3 to 3
- magnetic_y: float32 [512, 128, 1024], P('gx', 'gy', 'gz'), may hold values from -3 to 3
- magnetic_z: float32 [512, 128, 1024], P('gx', 'gy', 'gz'), may hold values from -3 to 3
- material: int32 [512, 128, 1024], P('gx', 'gy', 'gz'), may hold values from 0 to 15
- perm_table: float32 [16], replicated, may hold values from 1 to 12
Outputs:
- electric_x_half: float32 [512, 128, 1024], P('gx', 'gy', 'gz')
- electric_z_half: float32 [512, 128, 1024], P('gx', 'gy', 'gz')
The draws below stay inside these ranges and needn't reach their ends.
All inputs are finite; a program needn't handle non-finite values.
Results may differ from the reference program's by a relative error of at most 0.00021.
Values sent between devices are 32-bit elements; how exact they have to be, the bound alone decides.
No kernel may reach another device: no remote copies, remote signals or barrier semaphores. Data moves between devices by JAX's collectives and lax.ppermute only.
A program may use at most 192 MiB of HBM per device.

```python
import math
import jax
import jax.numpy as jnp
from jax import lax

NMAT = 16
NX = 512
NY = 128
NZ = 1024


def draw_electric_x(key, part):
    key = jax.random.fold_in(key, 11)
    grid_shape = (NX, NY, NZ)
    return jnp.clip(8.0 * jax.random.normal(key, grid_shape, jnp.float32), -32.0, 32.0)


def draw_electric_z(key, part):
    key = jax.random.fold_in(key, 23)
    grid_shape = (NX, NY, NZ)
    return jnp.clip(8.0 * jax.random.normal(key, grid_shape, jnp.float32), -32.0, 32.0)


def touch_ends(values, rng, smallest, high):
    index_at = [jax.random.randint(jax.random.fold_in(rng, axis), (), 0, length) for axis, length in enumerate(values.shape)]
    main_axis = values.shape.index(max(values.shape))
    beside = index_at[:main_axis] + [(index_at[main_axis] + 1) % values.shape[main_axis]] + index_at[main_axis + 1:]
    return values.at[tuple(index_at)].set(smallest).at[tuple(beside)].set(high)


def shard_levels(rng, dims, split, low, top_value):
    def one(dim, shards_of):
        draws = jax.random.uniform(jax.random.fold_in(jax.random.fold_in(rng, 6), dim), (shards_of,), jnp.float32, low / len(split), top_value / len(split))
        return jnp.repeat(jnp.exp(draws), dims[dim] // shards_of).reshape((-1,) + (1,) * (len(dims) - dim - 1))

    loudness = one(*split[0])
    for cut in split[1:]:
        loudness = loudness * one(*cut)
    return loudness


def normal_values(key, shape, width, most, split=(), dtype=jnp.bfloat16):
    array = jax.random.normal(key, shape, jnp.float32) * width
    if len(split) > 0:
        array = shard_levels(key, shape, split, -0.22, 0.18) * array
    return jnp.clip(array, min=-most, max=most).astype(dtype)


def setup_inputs(seed: int = 0) -> dict:
    streams_of = jax.random.split(jax.random.key(seed), 8)
    electric_x = draw_electric_x(jax.random.fold_in(streams_of[7], 71), 0)
    electric_z = draw_electric_z(jax.random.fold_in(streams_of[7], 71), 0)
    magnetic_x = normal_values(streams_of[2], (NX, NY, NZ), 0.5, 3.0, ((0, 16), (1, 8), (2, 2)), jnp.float32)
    magnetic_y = normal_values(streams_of[3], (NX, NY, NZ), 0.5, 3.0, ((0, 16), (1, 8), (2, 2)), jnp.float32)
    magnetic_z = normal_values(streams_of[4], (NX, NY, NZ), 0.5, 3.0, ((0, 16), (1, 8), (2, 2)), jnp.float32)
    material = touch_ends(jax.random.randint(streams_of[5], (NX, NY, NZ), 0, NMAT), jax.random.fold_in(streams_of[5], 1), 0, NMAT - 1).astype(jnp.int32)
    perm_table = jnp.clip(jnp.exp(jax.random.uniform(streams_of[6], (NMAT,), jnp.float32, math.log(1.0), math.log(12.0))), 1.0, 12.0)
    return dict(electric_x=electric_x, electric_z=electric_z, magnetic_x=magnetic_x, magnetic_y=magnetic_y, magnetic_z=magnetic_z, material=material, perm_table=perm_table)


def lower_diff(field_data, line_dim):
    widths = [(0, 0), (0, 0), (0, 0)]
    widths[line_dim] = (1, 0)
    padded = jnp.pad(field_data, widths)
    earlier = lax.slice_in_dim(padded, 0, field_data.shape[line_dim], axis=line_dim)
    return field_data - earlier

def solve_lines(source, line_ratio, line_dim):
    moved_source = jnp.moveaxis(source, line_dim, -1)
    moved_ratio = jnp.moveaxis(line_ratio, line_dim, -1)
    positions = jnp.arange(moved_ratio.shape[-1])
    lower_line = jnp.where(positions == 0, 0.0, -moved_ratio)
    upper_line = jnp.where(positions == moved_ratio.shape[-1] - 1, 0.0, -moved_ratio)
    main_line = 1.0 + 2.0 * moved_ratio
    solved = lax.linalg.tridiagonal_solve(lower_line, main_line, upper_line, moved_source[..., None])[..., 0]
    return jnp.moveaxis(solved, -1, line_dim)

def reference(electric_x, electric_z, magnetic_x, magnetic_y, magnetic_z, material, perm_table):
    permittivity = perm_table[material]
    curl_factor = 40.0 / permittivity
    line_ratio = 1600.0 / permittivity
    x_source = electric_x + curl_factor * (lower_diff(magnetic_z, 1) - lower_diff(magnetic_y, 2))
    z_source = electric_z + curl_factor * (lower_diff(magnetic_y, 0) - lower_diff(magnetic_x, 1))
    electric_x_half = solve_lines(x_source, line_ratio, 1)
    electric_z_half = solve_lines(z_source, line_ratio, 0)
    return (electric_x_half, electric_z_half)
```

```python
import functools

import jax
import jax.numpy as jnp
from jax import lax
from jax.experimental import pallas as pl
from jax.experimental.pallas import tpu as pltpu
from jax.sharding import PartitionSpec as P

ground_scale = 1.0 / 1600.0
drive_scale = 1.0 / 40.0
lane = 128
rows = 8
f32 = jnp.float32


def inverse(x):
    guess = pl.reciprocal(x, approx=True)
    return guess * (2.0 - x * guess)


def table_lookup(table, index):
    return jnp.take_along_axis(
        jnp.broadcast_to(table, index.shape), index, axis=1, mode="promise_in_bounds"
    )


def eliminate(state, ground, drive):
    link, left, here, left_drive, here_drive = state
    t = inverse(link + here + 1.0)
    next_link = link * t
    return (
        next_link,
        left + next_link * here,
        ground + here * t,
        left_drive + next_link * here_drive,
        drive + here_drive * t,
    ), t


def close_block(state, rim):
    link, left, here, left_drive, here_drive = state
    return (
        link,
        left,
        here,
        left_drive + link * rim,
        here_drive - (link + here + 1.0) * rim,
    )


def y_forward_kernel(
    table_ref, material_ref, ex_ref, my_ref, mz_ref, edge_ref,
    t_ref, drive_ref, rim_ref, reduced_ref, ground_s, drive_s, mz_s,
):
    xs, ys, zs = material_ref.shape
    tiles = zs // lane
    table = table_ref[...] * ground_scale
    lanes = lax.broadcasted_iota(jnp.int32, (xs * ys, lane), 1)
    before = pltpu.roll(edge_ref[...].reshape(xs * ys, lane), 1, 1)
    for k in range(tiles):
        cut = pl.ds(k * lane, lane)
        ground = table_lookup(table, material_ref[:, :, cut].reshape(xs * ys, lane))
        my = my_ref[:, :, cut].reshape(xs * ys, lane)
        rolled = pltpu.roll(my, 1, 1)
        lower = jnp.where(lanes == 0, before, rolled)
        before = rolled
        ground_s[k] = ground
        drive_s[k] = ground * ex_ref[:, :, cut].reshape(xs * ys, lane) - drive_scale * (my - lower)
        mz_s[k] = mz_ref[:, :, cut].reshape(xs * ys, lane)
    for k in range(tiles):
        cut = pl.ds(k * lane, lane)
        state = None
        last_mz = None
        for j in range(ys):
            pick = pl.ds(j, xs, stride=ys)
            ground = ground_s[k, pick, :]
            mz = drive_scale * mz_s[k, pick, :]
            drive = drive_s[k, pick, :] + mz
            if j == 0:
                state = (jnp.ones_like(ground), jnp.zeros_like(ground), ground, jnp.zeros_like(ground), drive)
            else:
                state, t = eliminate(state, ground, drive - last_mz)
                t_ref[j - 1, :, cut] = t
            drive_ref[j, :, cut] = state[4]
            last_mz = mz
        rim_ref[:, cut] = last_mz
        for v, value in enumerate(close_block(state, last_mz)):
            reduced_ref[k // 2, v, pl.ds((k % 2) * rows, rows), :] = value


def y_reduced_kernel(blocks_ref, ends_ref):
    count = blocks_ref.shape[0]
    block = [[blocks_ref[b, v] for v in range(5)] for b in range(count)]
    here = block[0][2] + block[0][0]
    drive = block[0][4]
    kept = []
    for b in range(1, count):
        link, left, right, left_drive, right_drive = block[b]
        total = here + left
        t = inverse(total + link)
        pull = link * t
        push = drive + left_drive
        kept.append((pull, push * t))
        here = right + pull * total
        drive = right_drive + pull * push
    value = drive * inverse(here + 1.0)
    ends_ref[count - 1, 1] = value
    for b in range(count - 1, 0, -1):
        pull, push = kept[b - 1]
        value = push + pull * value
        ends_ref[b, 0] = value
        ends_ref[b - 1, 1] = value
    ends_ref[0, 0] = jnp.zeros_like(value)


def y_back_kernel(t_ref, drive_ref, rim_ref, ends_ref, out_ref, out_s):
    ys, xs, zs = t_ref.shape
    for k in range(zs // lane):
        cut = pl.ds(k * lane, lane)
        half = pl.ds((k % 2) * rows, rows)
        before = ends_ref[k // 2, 0, half, :]
        value = ends_ref[k // 2, 1, half, :] + rim_ref[:, cut]
        reach = before
        parts = []
        for j in range(ys - 1):
            t = t_ref[j, :, cut]
            reach_t = reach * t
            parts.append((t, drive_ref[j, :, cut] * t + reach_t))
            reach = reach_t
        out_s[pl.ds(ys - 1, xs, stride=ys), :] = value
        for j in range(ys - 2, -1, -1):
            t, part = parts[j]
            value = part + t * value
            out_s[pl.ds(j, xs, stride=ys), :] = value
        out_ref[:, :, cut] = out_s[...].reshape(xs, ys, lane)


def x_forward_kernel(
    table_ref, material_ref, ez_ref, mx_ref, my_ref, edge_ref,
    t_ref, drive_ref, rim_ref, reduced_ref, state_s, last_my_s,
):
    xs, ys, zs = material_ref.shape
    step = pl.program_id(0)
    table = table_ref[...] * ground_scale
    row = lax.broadcasted_iota(jnp.int32, (ys, zs), 0)

    @pl.when(step == 0)
    def _():
        state_s[0] = jnp.zeros((ys, zs), f32)
        state_s[1] = jnp.zeros((ys, zs), f32)
        state_s[2] = jnp.zeros((ys, zs), f32)
        state_s[3] = jnp.zeros((ys, zs), f32)
        state_s[4] = jnp.zeros((ys, zs), f32)
        last_my_s[...] = jnp.zeros((ys, zs), f32)

    state = tuple(state_s[v] for v in range(5))
    last_my = last_my_s[...]
    for i in range(xs):
        index = material_ref[i]
        ground = jnp.concatenate(
            [table_lookup(table, index[:, k * lane:(k + 1) * lane]) for k in range(zs // lane)], axis=1
        )
        mx = mx_ref[i]
        lower_mx = jnp.where(row == 0, edge_ref[pl.ds(i, 1), :], pltpu.roll(mx, 1, 0))
        my = my_ref[i]
        drive = ground * ez_ref[i] + drive_scale * ((my - last_my) - (mx - lower_mx))
        last_my = my
        state, t = eliminate(state, ground, drive)
        if i == 0:
            first = step == 0
            link, left, here, left_drive, here_drive = state
            state = (jnp.where(first, 1.0, link), left, here, left_drive, here_drive)
        t_ref[i] = t
        drive_ref[i] = state[4]
    for v in range(5):
        state_s[v] = state[v]
    last_my_s[...] = last_my

    @pl.when(step == pl.num_programs(0) - 1)
    def _():
        rim = drive_scale * last_my
        rim_ref[...] = rim
        for v, value in enumerate(close_block(state, rim)):
            reduced_ref[v] = value


def x_back_kernel(t_ref, drive_ref, rim_ref, before_ref, here_ref, out_ref):
    xs = t_ref.shape[0]
    reach = before_ref[...]
    for i in range(xs - 1):
        t = t_ref[i + 1]
        reach = reach * t
        out_ref[i] = drive_ref[i] * t + reach
    value = here_ref[...] + rim_ref[...]
    out_ref[xs - 1] = value
    for i in range(xs - 2, -1, -1):
        value = out_ref[i] + t_ref[i + 1] * value
        out_ref[i] = value


def cost(elements, ops, arrays):
    return pl.CostEstimate(flops=elements * ops, bytes_accessed=elements * 4 * arrays, transcendentals=0)


def merge(a, b):
    total = a[2] + b[1]
    t = 1.0 / (total + a[0] + b[0])
    a_link, b_link = a[0] * t, b[0] * t
    push = a[4] + b[3]
    merged = jnp.stack(
        [
            a[0] * b_link,
            a[1] + a_link * total,
            b[2] + b_link * total,
            a[3] + a_link * push,
            b[4] + b_link * push,
        ]
    )
    return merged, (t * push, a_link, b_link)


def solve_along_x(own, axis):
    count = lax.axis_size(axis)
    place = lax.axis_index(axis)
    levels = []
    bit = 1
    while bit < count:
        mask = 3 * (bit // 2) if bit in (2, 8) else bit
        other = lax.ppermute(own, axis, [(i, i ^ mask) for i in range(count)])
        low = (place & bit) == 0
        own, solved = merge(jnp.where(low, own, other), jnp.where(low, other, own))
        levels.append((low, solved))
        bit *= 2
    before = jnp.zeros_like(own[0])
    here = own[4] / (own[2] + own[0] + 1.0)
    for low, (push, from_low, from_high) in reversed(levels):
        middle = push + from_low * before + from_high * here
        before, here = jnp.where(low, before, middle), jnp.where(low, middle, here)
    return before, here


def shift_up(x, axis):
    return lax.ppermute(x, axis, [(i, i + 1) for i in range(lax.axis_size(axis) - 1)])


def per_device(electric_x, electric_z, magnetic_x, magnetic_y, magnetic_z, material, perm_table):
    xs, ys, zs = material.shape
    chunks = xs // rows
    cells = xs * ys * zs
    sds = jax.ShapeDtypeStruct
    table = jnp.pad(perm_table, (0, lane - perm_table.shape[0])).reshape(1, lane)

    edge_z = shift_up(magnetic_y[:, :, zs - lane:], "gz")
    edge_y = shift_up(magnetic_x[:, ys - 1], "gy")

    slab = pl.BlockSpec((rows, ys, zs), lambda c: (c, 0, 0))
    turned = pl.BlockSpec((ys, rows, zs), lambda c: (0, c, 0))
    whole_table = pl.BlockSpec((1, lane), lambda c: (0, 0))
    vmem = pltpu.CompilerParams(vmem_limit_bytes=40 * 2**20)

    y_t, y_drive, y_rim, y_reduced = pl.pallas_call(
        y_forward_kernel,
        grid=(chunks,),
        in_specs=[whole_table, slab, slab, slab, slab, pl.BlockSpec((rows, ys, lane), lambda c: (c, 0, 0))],
        out_specs=[
            turned,
            turned,
            pl.BlockSpec((rows, zs), lambda c: (c, 0)),
            pl.BlockSpec((2, 5, 2 * rows, lane), lambda c: (c, 0, 0, 0)),
        ],
        out_shape=[
            sds((ys, xs, zs), f32),
            sds((ys, xs, zs), f32),
            sds((xs, zs), f32),
            sds((2 * chunks, 5, 2 * rows, lane), f32),
        ],
        scratch_shapes=[pltpu.VMEM((zs // lane, rows * ys, lane), f32)] * 3,
        compiler_params=vmem,
        cost_estimate=cost(cells, 30, 6),
        name="y_forward",
    )(table, material, electric_x, magnetic_y, magnetic_z, edge_z)

    y_blocks = lax.all_to_all(y_reduced, "gy", 0, 0, tiled=True)

    x_t, x_drive, x_rim, x_reduced = pl.pallas_call(
        x_forward_kernel,
        grid=(chunks,),
        in_specs=[whole_table, slab, slab, slab, slab, pl.BlockSpec((rows, zs), lambda c: (c, 0))],
        out_specs=[
            slab,
            slab,
            pl.BlockSpec((ys, zs), lambda c: (0, 0)),
            pl.BlockSpec((5, ys, zs), lambda c: (0, 0, 0)),
        ],
        out_shape=[
            sds((xs, ys, zs), f32),
            sds((xs, ys, zs), f32),
            sds((ys, zs), f32),
            sds((5, ys, zs), f32),
        ],
        scratch_shapes=[pltpu.VMEM((5, ys, zs), f32), pltpu.VMEM((ys, zs), f32)],
        compiler_params=vmem,
        cost_estimate=cost(cells, 30, 6),
        name="x_forward",
    )(table, material, electric_z, magnetic_x, magnetic_y, edge_y)

    x_before, x_here = solve_along_x(x_reduced, "gx")

    y_ends = pl.pallas_call(
        y_reduced_kernel,
        out_shape=sds((2 * chunks, 2, 2 * rows, lane), f32),
        compiler_params=vmem,
        cost_estimate=cost(y_blocks.size // 5, 20, 7),
        name="y_reduced",
    )(y_blocks)
    y_ends = lax.all_to_all(y_ends, "gy", 0, 0, tiled=True)

    electric_z_half = pl.pallas_call(
        x_back_kernel,
        out_shape=sds((xs, ys, zs), f32),
        compiler_params=vmem,
        cost_estimate=cost(cells, 5, 3),
        name="x_back",
    )(x_t, x_drive, x_rim, x_before, x_here)

    electric_x_half = pl.pallas_call(
        y_back_kernel,
        grid=(chunks,),
        in_specs=[
            turned,
            turned,
            pl.BlockSpec((rows, zs), lambda c: (c, 0)),
            pl.BlockSpec((2, 2, 2 * rows, lane), lambda c: (c, 0, 0, 0)),
        ],
        out_specs=slab,
        out_shape=sds((xs, ys, zs), f32),
        scratch_shapes=[pltpu.VMEM((rows * ys, lane), f32)],
        compiler_params=vmem,
        cost_estimate=cost(cells, 5, 3),
        name="y_back",
    )(y_t, y_drive, y_rim, y_ends)
    return (electric_x_half, electric_z_half)


def solution(mesh):
    field = P("gx", "gy", "gz")
    return jax.shard_map(
        per_device,
        mesh=mesh,
        in_specs=(field,) * 6 + (P(),),
        out_specs=(field, field),
        check_vma=False,
    )
```

```python
import functools

import jax
import jax.numpy as jnp
from jax import lax
from jax.experimental import pallas as pl
from jax.experimental.pallas import tpu as pltpu
from jax.sharding import PartitionSpec as P

ground_scale = 1.0 / 1600.0
drive_scale = 1.0 / 40.0
lane = 128
rows = 8
pair = 2
long = 8
hold_bit = 2
f32 = jnp.float32


def inverse(x):
    return pltpu.reciprocal(x, approx=True)


def table_lookup(table, index):
    return jnp.take_along_axis(
        jnp.broadcast_to(table, index.shape), index, axis=1, mode="promise_in_bounds"
    )


def eliminate(state, ground, drive):
    link, left, here, left_drive, here_drive = state
    t = inverse(link + here + 1.0)
    next_link = link * t
    return (
        next_link,
        left + next_link * here,
        ground + here * t,
        left_drive + next_link * here_drive,
        drive + here_drive * t,
    ), t


def close_block(state, rim):
    link, left, here, left_drive, here_drive = state
    return (
        link,
        left,
        here,
        left_drive + link * rim,
        here_drive - (link + here + 1.0) * rim,
    )


def forward_kernel(
    table_ref, material_ref, ex_ref, ez_ref, mx_ref, my_ref, mz_ref, edge_ref,
    yt_ref, ydrive_ref, yreduced_ref, xt_ref, xdrive_ref, xreduced_ref, t_edge_ref,
    ground_s, drive_s, state_s, my_s,
):
    xs, ys, zs = material_ref.shape
    step = pl.program_id(0)
    tiles = zs // lane
    flat = (xs * ys, lane)
    table = table_ref[...] * ground_scale
    first_lane = lax.broadcasted_iota(jnp.int32, flat, 1) == 0
    first_y = lax.broadcasted_iota(jnp.int32, (xs, ys, lane), 1) == 0
    first_cell = step == 0

    @pl.when(first_cell)
    def _():
        state_s[...] = jnp.zeros_like(state_s)
        my_s[...] = jnp.zeros_like(my_s)

    before = pltpu.roll(edge_ref[...].reshape(flat), 1, 1)
    for k in range(tiles):
        cut = pl.ds(k * lane, lane)
        ground = table_lookup(table, material_ref[:, :, cut].reshape(flat))
        my = my_ref[:, :, cut]
        rolled = pltpu.roll(my.reshape(flat), 1, 1)
        my_step = my.reshape(flat) - jnp.where(first_lane, before, rolled)
        before = rolled
        mz = mz_ref[:, :, cut]
        mz_step = mz - jnp.where(first_y, 0.0, pltpu.roll(mz, 1, 1))
        ground_s[k] = ground
        drive_s[k] = ground * ex_ref[:, :, cut].reshape(flat) + drive_scale * (mz_step.reshape(flat) - my_step)
        mx = mx_ref[:, :, cut]
        mx_step = mx - jnp.where(first_y, 0.0, pltpu.roll(mx, 1, 1))

        state = tuple(state_s[v, :, cut] for v in range(5))
        last_my = my_s[:, cut]
        ground = ground.reshape(xs, ys, lane)
        for i in range(xs):
            drive = ground[i] * ez_ref[i, :, cut] + drive_scale * ((my[i] - last_my) - mx_step[i])
            last_my = my[i]
            state, t = eliminate(state, ground[i], drive)
            if i == 0:
                state = (jnp.where(first_cell, 1.0, state[0]),) + state[1:]
            xt_ref[i, :, cut] = t
            t_edge_ref[pl.ds(i, 1), cut] = t[0:1]
            xdrive_ref[i, :, cut] = state[4]
        for v in range(5):
            state_s[v, :, cut] = state[v]
        my_s[:, cut] = last_my
        rim = drive_scale * last_my

        @pl.when(step == pl.num_programs(0) - 1)
        def _(rim=rim, cut=cut):
            xdrive_ref[xs - 1, :, cut] = rim

        for v, value in enumerate(close_block(state, rim)):
            xreduced_ref[v, :, cut] = value
        if k % pair == pair - 1:
            y_eliminate(range(k - pair + 1, k + 1), mz_ref, yt_ref, ydrive_ref, yreduced_ref, ground_s, drive_s)


kept_count = 13


def x_edge_kernel(edge_ref, t_ref, reduced_ref, reduced_out, kept_ref):
    xs = t_ref.shape[0]
    row = pl.ds(0, 1)
    here = drive_scale * edge_ref[row, :]
    link = jnp.ones_like(here)
    left = jnp.zeros_like(here)
    kept_ref[11, row, :] = here
    for i in range(1, xs):
        t = t_ref[pl.ds(i, 1), :]
        link = link * t
        left = left + link * here
        here = drive_scale * edge_ref[pl.ds(i, 1), :] + here * t
        kept_ref[11 + i // 16, pl.ds(i % 16, 1), :] = here
    for v in range(5):
        reduced_out[v] = reduced_ref[v]
    reduced_out[3, row, :] = reduced_ref[3, row, :] + left
    reduced_out[4, row, :] = reduced_ref[4, row, :] + here


def y_eliminate(tiles, mz_ref, t_ref, drive_ref, reduced_ref, ground_s, drive_s):
    xs, ys, _ = mz_ref.shape
    for c in range(xs // rows):
        here = (pl.ds(c * rows, rows), pl.ds(tiles[0] * lane, pair * lane))
        state = None
        for j in range(ys):
            pick = pl.ds(c * rows * ys + j, rows, stride=ys)
            ground = jnp.concatenate([ground_s[k, pick, :] for k in tiles], axis=1)
            drive = jnp.concatenate([drive_s[k, pick, :] for k in tiles], axis=1)
            if j == 0:
                zero = jnp.zeros_like(ground)
                state = (jnp.ones_like(ground), zero, ground, zero, drive)
            else:
                state, t = eliminate(state, ground, drive)
                t_ref[(j - 1,) + here] = t
            if j < ys - 1:
                drive_ref[(j,) + here] = state[4]
        rim = drive_scale * mz_ref[here[0], ys - 1, here[1]]
        drive_ref[(ys - 1,) + here] = rim
        for v, value in enumerate(close_block(state, rim)):
            for n, k in enumerate(tiles):
                reduced_ref[2 * c + k // 2, v, pl.ds((k % 2) * rows, rows), :] = value[:, n * lane:(n + 1) * lane]


def y_reduced_kernel(blocks_ref, ends_ref):
    count = blocks_ref.shape[0]
    block = [[blocks_ref[b, v] for v in range(5)] for b in range(count)]
    here = block[0][2] + block[0][0]
    drive = block[0][4]
    kept = []
    for b in range(1, count):
        link, left, right, left_drive, right_drive = block[b]
        total = here + left
        t = inverse(total + link)
        pull = link * t
        push = drive + left_drive
        kept.append((pull, push * t))
        here = right + pull * total
        drive = right_drive + pull * push
    value = drive * inverse(here + 1.0)
    ends_ref[count - 1, 1] = value
    for b in range(count - 1, 0, -1):
        pull, push = kept[b - 1]
        value = push + pull * value
        ends_ref[b, 0] = value
        ends_ref[b - 1, 1] = value
    ends_ref[0, 0] = jnp.zeros_like(value)


def y_back_kernel(t_ref, drive_ref, ends_ref, out_ref, out_s):
    ys, xs, zs = t_ref.shape
    for k in range(zs // lane):
        cut = pl.ds(k * lane, lane)
        half = pl.ds((k % 2) * rows, rows)
        before = ends_ref[k // 2, 0, half, :]
        value = ends_ref[k // 2, 1, half, :] + drive_ref[ys - 1, :, cut]
        reach = before
        parts = []
        for j in range(ys - 1):
            t = t_ref[j, :, cut]
            reach_t = reach * t
            parts.append((t, drive_ref[j, :, cut] * t + reach_t))
            reach = reach_t
        out_s[pl.ds(ys - 1, xs, stride=ys), :] = value
        for j in range(ys - 2, -1, -1):
            t, part = parts[j]
            value = part + t * value
            out_s[pl.ds(j, xs, stride=ys), :] = value
        out_ref[:, :, cut] = out_s[...].reshape(xs, ys, lane)


def x_back_kernel(low_ref, t_ref, drive_ref, kept_ref, side_ref, other_ref, out_ref):
    xs, ys, zs = t_ref.shape
    top = low_ref[3] == 1
    middle = (side_ref[1] + other_ref[1]) * inverse(side_ref[0] + other_ref[0])
    before = jnp.where(top, 0.0, middle)
    here = jnp.where(top, middle, kept_ref[9] + kept_ref[10] * middle)
    for level in (2, 1, 0):
        low = low_ref[level] == 1
        middle = kept_ref[3 * level] + kept_ref[3 * level + 1] * before + kept_ref[3 * level + 2] * here
        before, here = jnp.where(low, before, middle), jnp.where(low, middle, here)
    first_y = lax.broadcasted_iota(jnp.int32, (ys, zs), 0) == 0
    reach = before
    for i in range(xs - 1):
        t = t_ref[i + 1]
        edge = jnp.where(first_y, kept_ref[11 + i // 16, pl.ds(i % 16, 1), :], 0.0)
        reach = reach * t
        out_ref[i] = (drive_ref[i] + edge) * t + reach
    value = here + drive_ref[xs - 1]
    out_ref[xs - 1] = value
    for i in range(xs - 2, -1, -1):
        value = out_ref[i] + t_ref[i + 1] * value
        out_ref[i] = value


def cost(elements, ops, arrays):
    return pl.CostEstimate(flops=elements * ops, bytes_accessed=elements * 4 * arrays, transcendentals=0)


def merge(low, own_ref, other_ref, kept_ref, slot):
    own = [own_ref[v] for v in range(5)]
    other = [other_ref[v] for v in range(5)]
    a = [jnp.where(low, p, q) for p, q in zip(own, other)]
    b = [jnp.where(low, q, p) for p, q in zip(own, other)]
    total = a[2] + b[1]
    t = inverse(total + a[0] + b[0])
    a_link, b_link = a[0] * t, b[0] * t
    push = a[4] + b[3]
    kept_ref[slot] = push * t
    kept_ref[slot + 1] = a_link
    kept_ref[slot + 2] = b_link
    return (
        a[0] * b_link,
        a[1] + a_link * total,
        b[2] + b_link * total,
        a[3] + a_link * push,
        b[4] + b_link * push,
    )


def merge_kernel(level, low_ref, own_ref, other_ref, _, merged_ref, kept_ref):
    merged = merge(low_ref[level] == 1, own_ref, other_ref, kept_ref, 3 * level)
    for v in range(5):
        merged_ref[v] = merged[v]


def last_merge_kernel(low_ref, own_ref, other_ref, _, side_ref, kept_ref):
    link, left, right, left_drive, right_drive = merge(low_ref[2] == 1, own_ref, other_ref, kept_ref, 6)
    closed = inverse(right + link + 1.0)
    share = link * closed
    top = low_ref[3] == 1
    side_ref[0] = jnp.where(top, right + link, left + share * (right + 1.0))
    side_ref[1] = jnp.where(top, right_drive, left_drive + share * right_drive)
    kept_ref[9] = closed * right_drive
    kept_ref[10] = share


def exchange(x, axis, mask):
    return lax.ppermute(x, axis, [(i, i ^ mask) for i in range(lax.axis_size(axis))])


def in_vmem(a):
    return pltpu.with_memory_space_constraint(a, pltpu.VMEM)


def merge_call(kernel, low, own, other, kept, size):
    _, ys, zs = own.shape
    whole = pl.BlockSpec(memory_space=pltpu.VMEM)
    return pl.pallas_call(
        kernel,
        in_specs=[pl.BlockSpec(memory_space=pltpu.SMEM)] + [whole] * 3,
        out_specs=[whole] * 2,
        out_shape=[pltpu.VMEM((size, ys, zs), f32), pltpu.VMEM(kept.shape, f32)],
        input_output_aliases={3: 1},
        compiler_params=pltpu.CompilerParams(vmem_limit_bytes=8 * 2**20),
        cost_estimate=cost(own.size, 10, 3),
        name="x_merge",
    )(low, in_vmem(own), in_vmem(other), in_vmem(kept))


def load_kernel(t_ref, drive_ref, _, t_out, drive_out, sems):
    copies = [
        pltpu.make_async_copy(t_ref, t_out, sems.at[0]),
        pltpu.make_async_copy(drive_ref, drive_out, sems.at[1]),
    ]
    for copy in copies:
        copy.start()
    for copy in copies:
        copy.wait()


def load(t, drive, after):
    in_hbm_spec = pl.BlockSpec(memory_space=pltpu.HBM)
    whole = pl.BlockSpec(memory_space=pltpu.VMEM)
    return pl.pallas_call(
        load_kernel,
        in_specs=[in_hbm_spec] * 2 + [pl.BlockSpec(memory_space=pl.ANY)],
        out_specs=[whole] * 2,
        out_shape=[pltpu.VMEM(t.shape, f32)] * 2,
        scratch_shapes=[pltpu.SemaphoreType.DMA((2,))],
        compiler_params=pltpu.CompilerParams(vmem_limit_bytes=8 * 2**20),
        cost_estimate=cost(t.size, 1, 4),
        name="load",
    )(*(pltpu.with_memory_space_constraint(a, pltpu.HBM) for a in (t, drive)), after)


def shift_up(x, axis):
    return lax.ppermute(x, axis, [(i, i + 1) for i in range(lax.axis_size(axis) - 1)])


def per_device(electric_x, electric_z, magnetic_x, magnetic_y, magnetic_z, material, perm_table):
    xs, ys, zs = material.shape
    chunks = xs // rows
    cells = xs * ys * zs
    sds = jax.ShapeDtypeStruct
    table = jnp.pad(perm_table, (0, lane - perm_table.shape[0])).reshape(1, lane)

    edge_z = shift_up(magnetic_y[:, :, zs - lane:], "gz")
    edge_y = shift_up(magnetic_x[:, ys - 1], "gy")

    def in_hbm(a):
        return pltpu.with_memory_space_constraint(a, pltpu.HBM)

    slab = pl.BlockSpec((rows, ys, zs), lambda c: (c, 0, 0))
    turned = pl.BlockSpec((ys, rows, zs), lambda c: (0, c, 0))
    long_slab = pl.BlockSpec((long, ys, zs), lambda c: (c, 0, 0))
    long_turned = pl.BlockSpec((ys, long, zs), lambda c: (0, c, 0))
    whole_table = pl.BlockSpec((1, lane), lambda c: (0, 0))
    vmem = pltpu.CompilerParams(vmem_limit_bytes=24 * 2**20)

    y_t, y_drive, y_reduced, x_t, x_drive, x_reduced, t_edge = pl.pallas_call(
        forward_kernel,
        grid=(xs // long,),
        in_specs=[whole_table] + [long_slab] * 6 + [pl.BlockSpec((long, ys, lane), lambda c: (c, 0, 0))],
        out_specs=[
            long_turned,
            long_turned,
            pl.BlockSpec((long // 4, 5, 2 * rows, lane), lambda c: (c, 0, 0, 0)),
            long_slab,
            long_slab,
            pl.BlockSpec((5, ys, zs), lambda c: (0, 0, 0)),
            pl.BlockSpec((long, zs), lambda c: (c, 0)),
        ],
        out_shape=[
            pltpu.HBM((ys, xs, zs), f32),
            pltpu.HBM((ys, xs, zs), f32),
            pltpu.HBM((2 * chunks, 5, 2 * rows, lane), f32),
            pltpu.HBM((xs, ys, zs), f32),
            pltpu.HBM((xs, ys, zs), f32),
            pltpu.VMEM((5, ys, zs), f32),
            pltpu.VMEM((xs, zs), f32),
        ],
        scratch_shapes=[pltpu.VMEM((zs // lane, long * ys, lane), f32)] * 2
        + [pltpu.VMEM((5, ys, zs), f32), pltpu.VMEM((ys, zs), f32)],
        compiler_params=vmem,
        cost_estimate=cost(cells, 60, 10),
        name="forward",
    )(
        table, in_hbm(material), in_hbm(electric_x), in_hbm(electric_z), in_hbm(magnetic_x),
        in_hbm(magnetic_y), in_hbm(magnetic_z), edge_z,
    )

    y_reduced, edge_y = lax.optimization_barrier((y_reduced, edge_y))
    y_blocks = lax.all_to_all(y_reduced, "gy", 0, 0, tiled=True)

    in_place = pl.BlockSpec(memory_space=pltpu.VMEM)
    x_reduced, kept = pl.pallas_call(
        x_edge_kernel,
        in_specs=[in_place] * 3,
        out_specs=[in_place] * 2,
        out_shape=[pltpu.VMEM((5, ys, zs), f32), pltpu.VMEM((kept_count, ys, zs), f32)],
        compiler_params=vmem,
        cost_estimate=cost(cells // ys, 10, 3),
        name="x_edge",
    )(edge_y, t_edge, x_reduced)

    y_ends = pl.pallas_call(
        y_reduced_kernel,
        out_shape=pltpu.HBM((2 * chunks, 2, 2 * rows, lane), f32),
        compiler_params=vmem,
        cost_estimate=cost(y_blocks.size // 5, 20, 7),
        name="y_reduced",
    )(y_blocks)

    hold_level = 1
    place = lax.axis_index("gx")
    low = jnp.stack([((place & bit) == 0).astype(jnp.int32) for bit in (1, 2, 4, 8)])
    own = x_reduced
    for level, mask in enumerate((1, 3, 4)):
        other = exchange(own, "gx", mask)
        if level == hold_level:
            other, y_ends = lax.optimization_barrier((other, y_ends))
        kernel = functools.partial(merge_kernel, level) if level < 2 else last_merge_kernel
        own, kept = merge_call(kernel, low, own, other, kept, 5 if level < 2 else 2)
    x_t, x_drive = load(x_t, x_drive, own)
    side_other = exchange(own, "gx", 12)
    y_t, y_drive = load(y_t, y_drive, y_ends)
    y_ends = lax.all_to_all(y_ends, "gy", 0, 0, tiled=True)

    electric_z_half = pl.pallas_call(
        x_back_kernel,
        in_specs=[pl.BlockSpec(memory_space=pltpu.SMEM)] + [pl.BlockSpec(memory_space=pltpu.VMEM)] * 5,
        out_shape=sds((xs, ys, zs), f32),
        compiler_params=vmem,
        cost_estimate=cost(cells, 5, 3),
        name="x_back",
    )(low, *map(in_vmem, (x_t, x_drive, kept, own, side_other)))

    electric_x_half = pl.pallas_call(
        y_back_kernel,
        grid=(chunks,),
        in_specs=[
            turned,
            turned,
            pl.BlockSpec((2, 2, 2 * rows, lane), lambda c: (c, 0, 0, 0)),
        ],
        out_specs=slab,
        out_shape=sds((xs, ys, zs), f32),
        scratch_shapes=[pltpu.VMEM((rows * ys, lane), f32)],
        compiler_params=vmem,
        cost_estimate=cost(cells, 5, 3),
        name="y_back",
    )(in_vmem(y_t), in_vmem(y_drive), y_ends)
    return (electric_x_half, electric_z_half)


def solution(mesh):
    field = P("gx", "gy", "gz")
    return jax.shard_map(
        per_device,
        mesh=mesh,
        in_specs=(field,) * 6 + (P(),),
        out_specs=(field, field),
        check_vma=False,
    )
```

```python
import functools

import jax
import jax.numpy as jnp
from jax import lax
from jax.experimental import pallas as pl
from jax.experimental.pallas import tpu as pltpu
from jax.sharding import PartitionSpec as P

ground_scale = 1.0 / 1600.0
drive_scale = 1.0 / 40.0
lane = 128
rows = 8
f32 = jnp.float32
vmem_spec = pl.BlockSpec(memory_space=pltpu.VMEM)
smem_spec = pl.BlockSpec(memory_space=pltpu.SMEM)
hbm_spec = pl.BlockSpec(memory_space=pltpu.HBM)


def inverse(x):
    return pltpu.reciprocal(x, approx=True)


def eliminate(state, ground, drive):
    link, left, here, left_drive, here_drive = state
    t = inverse(link + here + 1.0)
    next_link = link * t
    return (
        next_link,
        left + next_link * here,
        ground + here * t,
        left_drive + next_link * here_drive,
        drive + here_drive * t,
    ), t


def close_block(state, rim):
    link, left, here, left_drive, here_drive = state
    return (
        link,
        left,
        here,
        left_drive + link * rim,
        here_drive - (link + here + 1.0) * rim,
    )


def forward_kernel(
    table_hbm, material_hbm, ex_hbm, ez_hbm, mx_hbm, my_hbm, mz_hbm,
    yt_ref, ydrive_ref, yreduced_ref, xt_hbm, xdrive_hbm, xreduced_ref,
    yt_edge_ref, my_edge_ref, xt_edge_ref, mx_edge_ref,
    table_s, material_s, ex_s, ez_s, mx_s, my_s, mz_s, xt_s, xjs_s, ground_s, ydrive_s, xdrive_s, turn_s,
    state_s, last_my_s, table_sem, sems, out_sems,
):
    xs, ys, zs = material_s.shape
    tiles = zs // lane
    chunks = xs // rows
    flat = (rows * ys, lane)
    cube = (rows, ys, lane)
    arrays = (
        (material_hbm, material_s), (my_hbm, my_s), (mz_hbm, mz_s),
        (ex_hbm, ex_s), (ez_hbm, ez_s), (mx_hbm, mx_s),
    )

    def chunk_copies(c):
        part = pl.ds(pl.multiple_of(c * rows, rows), rows)
        return [
            pltpu.make_async_copy(source.at[part], target.at[part], sems.at[a, c])
            for a, (source, target) in enumerate(arrays)
        ]

    def chunk_stores(c):
        part = pl.ds(pl.multiple_of(c * rows, rows), rows)
        return [
            pltpu.make_async_copy(source.at[part], target.at[part], out_sems.at[a, c])
            for a, (source, target) in enumerate(((xt_s, xt_hbm), (xjs_s, xdrive_hbm)))
        ]

    table_copy = pltpu.make_async_copy(table_hbm, table_s, table_sem)
    table_copy.start()
    for c in range(chunks):
        for copy in chunk_copies(c):
            copy.start()
    lanes = lax.broadcasted_iota(jnp.int32, flat, 1)
    first_lane = lanes == 0
    first_y = lax.broadcasted_iota(jnp.int32, cube, 1) == 0
    edge_lanes = lax.broadcasted_iota(jnp.int32, (rows, lane), 1)
    my_edge_ref[...] = jnp.zeros_like(my_edge_ref)
    state_s[...] = jnp.zeros_like(state_s)
    last_my_s[...] = jnp.zeros_like(last_my_s)
    table_copy.wait()
    table = jnp.zeros((1, lane), f32)
    for m in range(table_s.shape[0]):
        table = jnp.where(lax.broadcasted_iota(jnp.int32, (1, lane), 1) == m, table_s[m], table)
    table = table * ground_scale

    def chunk(c, _):
        for copy in chunk_copies(c):
            copy.wait()
        part = pl.ds(pl.multiple_of(c * rows, rows), rows)
        before = jnp.zeros(flat, f32)
        for k in range(tiles):
            cut = pl.ds(k * lane, lane)
            ground = jnp.take_along_axis(
                jnp.broadcast_to(table, flat), material_s[part, :, cut].reshape(flat), axis=1, mode="promise_in_bounds"
            )
            my = my_s[part, :, cut]
            rolled = pltpu.roll(my.reshape(flat), 1, 1)
            my_step = my.reshape(flat) - jnp.where(first_lane, before, rolled)
            before = rolled
            mz = mz_s[part, :, cut]
            mz_step = (mz - jnp.where(first_y, 0.0, pltpu.roll(mz, 1, 1))).reshape(flat)
            mx = mx_s[part, :, cut]
            mx_step = (mx - jnp.where(first_y, 0.0, pltpu.roll(mx, 1, 1))).reshape(flat)
            my_up = (my - jnp.concatenate([last_my_s[:, cut][None], my[:-1]], axis=0)).reshape(flat)
            last_my_s[:, cut] = my[rows - 1]
            ground_s[k] = ground
            ydrive_s[k] = ground * ex_s[part, :, cut].reshape(flat) + drive_scale * (mz_step - my_step)
            xdrive_s[k] = ground * ez_s[part, :, cut].reshape(flat) + drive_scale * (my_up - mx_step)
            mx_edge_ref[part, cut] = mx_s[part, ys - 1, cut]
            if k == tiles - 1:
                turn_s[...] = my.reshape(flat)

        states = [tuple(state_s[v, :, pl.ds(k * lane, lane)] for v in range(5)) for k in range(tiles)]
        for i in range(rows):
            line = pl.ds(i * ys, ys)
            for k in range(tiles):
                cut = pl.ds(k * lane, lane)
                state, t = eliminate(states[k], ground_s[k, line, :], xdrive_s[k, line, :])
                if i == 0:
                    state = (jnp.where(c == 0, 1.0, state[0]),) + state[1:]
                states[k] = state
                xt_s[c * rows + i, :, cut] = t
                js = state[4]
                if i == rows - 1:
                    js = jnp.where(c == chunks - 1, drive_scale * last_my_s[:, cut], js)
                xjs_s[c * rows + i, :, cut] = js
                xt_edge_ref[c * rows + i, :, cut] = t[0:1]
        for k in range(tiles):
            for v in range(5):
                state_s[v, :, pl.ds(k * lane, lane)] = states[k][v]
        for copy in chunk_stores(c):
            copy.start()

        for first in range(0, tiles, 2):
            pair = (first, first + 1)
            states = [None, None]
            for j in range(ys):
                pick = pl.ds(j, rows, stride=ys)
                for n, k in enumerate(pair):
                    cut = pl.ds(k * lane, lane)
                    ground = ground_s[k, pick, :]
                    drive = ydrive_s[k, pick, :]
                    if j == 0:
                        zero = jnp.zeros_like(ground)
                        states[n] = (jnp.ones_like(ground), zero, ground, zero, drive)
                    else:
                        states[n], t = eliminate(states[n], ground, drive)
                        yt_ref[j - 1, part, cut] = t
                        if k == 0:
                            yt_edge_ref[j - 1, part, :] = t
                    if j < ys - 1:
                        ydrive_ref[j, part, cut] = states[n][4]
            for n, k in enumerate(pair):
                cut = pl.ds(k * lane, lane)
                rim = drive_scale * mz_s[part, ys - 1, cut]
                ydrive_ref[ys - 1, part, cut] = rim
                for v, value in enumerate(close_block(states[n], rim)):
                    yreduced_ref[2 * c + k // 2, v, pl.ds((k % 2) * rows, rows), :] = value
        packed = my_edge_ref[...]
        for j in range(ys):
            place = j * chunks + c
            turned = pltpu.roll(turn_s[pl.ds(j, rows, stride=ys), :], place + 1, 1)
            packed = jnp.where(edge_lanes == place, turned, packed)
        my_edge_ref[...] = packed
        return _

    lax.fori_loop(0, chunks, chunk, 0)
    rim = drive_scale * last_my_s[...]
    for v, value in enumerate(close_block(tuple(state_s[v] for v in range(5)), rim)):
        xreduced_ref[v] = value
    for c in range(chunks):
        for copy in chunk_stores(c):
            copy.wait()


def y_edge_kernel(edge_ref, t_ref, reduced_ref, drive_ref, reduced_out, drive_out):
    ys, xs, _ = t_ref.shape
    reduced_out[...] = reduced_ref[...]
    first_lane = lax.broadcasted_iota(jnp.int32, (rows, lane), 1) == 0
    for c in range(xs // rows):
        part = pl.ds(c * rows, rows)

        def rim(j, c=c):
            place = j * (xs // rows) + c
            turned = pltpu.roll(edge_ref[...], (lane - place) % lane, 1)
            return jnp.where(first_lane, drive_scale * turned, 0.0)

        here = rim(0)
        link = jnp.ones_like(here)
        left = jnp.zeros_like(here)
        for j in range(ys):
            if j > 0:
                t = t_ref[j - 1, part, :]
                link = link * t
                left = left + link * here
                here = rim(j) + here * t
            if j < ys - 1:
                drive_out[j, part, pl.ds(0, lane)] = drive_ref[j, part, pl.ds(0, lane)] + here
        reduced_out[2 * c, 3, pl.ds(0, rows), :] = reduced_ref[2 * c, 3, pl.ds(0, rows), :] + left
        reduced_out[2 * c, 4, pl.ds(0, rows), :] = reduced_ref[2 * c, 4, pl.ds(0, rows), :] + here


kept_count = 13


def x_edge_kernel(edge_ref, t_ref, reduced_ref, reduced_out, kept_ref):
    xs = t_ref.shape[0]
    ys = reduced_ref.shape[1]
    row = pl.ds(0, 1)
    here = drive_scale * edge_ref[row, :]
    link = jnp.ones_like(here)
    left = jnp.zeros_like(here)
    kept_ref[11, row, :] = here
    for i in range(1, xs):
        t = t_ref[i]
        link = link * t
        left = left + link * here
        here = drive_scale * edge_ref[pl.ds(i, 1), :] + here * t
        kept_ref[11 + i // ys, pl.ds(i % ys, 1), :] = here
    for v in range(5):
        reduced_out[v] = reduced_ref[v]
    reduced_out[3, row, :] = reduced_ref[3, row, :] + left
    reduced_out[4, row, :] = reduced_ref[4, row, :] + here


def y_reduced_kernel(blocks_ref, ends_ref):
    count = blocks_ref.shape[0]
    block = [[blocks_ref[b, v] for v in range(5)] for b in range(count)]
    here = block[0][2] + block[0][0]
    drive = block[0][4]
    kept = []
    for b in range(1, count):
        link, left, right, left_drive, right_drive = block[b]
        total = here + left
        t = inverse(total + link)
        pull = link * t
        push = drive + left_drive
        kept.append((pull, push * t))
        here = right + pull * total
        drive = right_drive + pull * push
    value = drive * inverse(here + 1.0)
    ends_ref[count - 1, 1] = value
    for b in range(count - 1, 0, -1):
        pull, push = kept[b - 1]
        value = push + pull * value
        ends_ref[b, 0] = value
        ends_ref[b - 1, 1] = value
    ends_ref[0, 0] = jnp.zeros_like(value)


def merge(low, own_ref, other_ref, kept_ref, slot):
    own = [own_ref[v] for v in range(5)]
    other = [other_ref[v] for v in range(5)]
    a = [jnp.where(low, p, q) for p, q in zip(own, other)]
    b = [jnp.where(low, q, p) for p, q in zip(own, other)]
    total = a[2] + b[1]
    t = inverse(total + a[0] + b[0])
    a_link, b_link = a[0] * t, b[0] * t
    push = a[4] + b[3]
    kept_ref[slot] = push * t
    kept_ref[slot + 1] = a_link
    kept_ref[slot + 2] = b_link
    return (
        a[0] * b_link,
        a[1] + a_link * total,
        b[2] + b_link * total,
        a[3] + a_link * push,
        b[4] + b_link * push,
    )


def is_low(level):
    return (lax.axis_index("gx") >> level) & 1 == 0


def merge_kernel(level, own_ref, other_ref, _, merged_ref, kept_ref):
    merged = merge(is_low(level), own_ref, other_ref, kept_ref, 3 * level)
    for v in range(5):
        merged_ref[v] = merged[v]


def last_merge_kernel(level, own_ref, other_ref, _, side_ref, kept_ref):
    link, left, right, left_drive, right_drive = merge(is_low(level), own_ref, other_ref, kept_ref, 3 * level)
    closed = inverse(right + link + 1.0)
    share = link * closed
    top = is_low(level + 1)
    side_ref[0] = jnp.where(top, right + link, left + share * (right + 1.0))
    side_ref[1] = jnp.where(top, right_drive, left_drive + share * right_drive)
    kept_ref[9] = closed * right_drive
    kept_ref[10] = share


def y_back_kernel(
    t_ref, drive_ref, ends_ref, xt_hbm, xdrive_hbm, out_hbm, xt_ref, xdrive_ref, turn_s, out_s, sems, load_sems
):
    loads = [
        pltpu.make_async_copy(xt_hbm, xt_ref, load_sems.at[0]),
        pltpu.make_async_copy(xdrive_hbm, xdrive_ref, load_sems.at[1]),
    ]
    for load in loads:
        load.start()
    ys, xs, zs = t_ref.shape
    copies = []
    for c in range(xs // rows):
        part = pl.ds(c * rows, rows)
        for k in range(zs // lane):
            cut = pl.ds(k * lane, lane)
            half = pl.ds((k % 2) * rows, rows)
            reach = ends_ref[2 * c + k // 2, 0, half, :]
            value = ends_ref[2 * c + k // 2, 1, half, :] + drive_ref[ys - 1, part, cut]
            parts = []
            for j in range(ys - 1):
                t = t_ref[j, part, cut]
                reach = reach * t
                parts.append((t, drive_ref[j, part, cut] * t + reach))
            turn_s[k, pl.ds(ys - 1, rows, stride=ys), :] = value
            for j in range(ys - 2, -1, -1):
                t, share = parts[j]
                value = share + t * value
                turn_s[k, pl.ds(j, rows, stride=ys), :] = value
            out_s[part, :, cut] = turn_s[k].reshape(rows, ys, lane)
        copies.append(pltpu.make_async_copy(out_s.at[part], out_hbm.at[part], sems.at[c]))
        copies[-1].start()
    for copy in copies + loads:
        copy.wait()


def x_back_kernel(t_ref, drive_ref, kept_ref, side_ref, other_ref, out_ref):
    xs, ys, zs = t_ref.shape
    top = is_low(3)
    middle = (side_ref[1] + other_ref[1]) * inverse(side_ref[0] + other_ref[0])
    before = jnp.where(top, 0.0, middle)
    here = jnp.where(top, middle, kept_ref[9] + kept_ref[10] * middle)
    for level in (2, 1, 0):
        low = is_low(level)
        middle = kept_ref[3 * level] + kept_ref[3 * level + 1] * before + kept_ref[3 * level + 2] * here
        before, here = jnp.where(low, before, middle), jnp.where(low, middle, here)
    first_y = lax.broadcasted_iota(jnp.int32, (ys, zs), 0) == 0
    reach = before
    for i in range(xs - 1):
        t = t_ref[i + 1]
        reach = reach * t
        edge = jnp.where(first_y, kept_ref[11 + i // ys, pl.ds(i % ys, 1), :], 0.0)
        out_ref[i] = (drive_ref[i] + edge) * t + reach
    value = here + drive_ref[xs - 1]
    out_ref[xs - 1] = value
    for i in range(xs - 2, -1, -1):
        value = out_ref[i] + t_ref[i + 1] * value
        out_ref[i] = value


def cost(elements, ops, arrays):
    return pl.CostEstimate(flops=elements * ops, bytes_accessed=elements * 4 * arrays, transcendentals=0)


def call(kernel, name, inputs, outs, carried=(), limit=16, work=None, scratch=()):
    specs = [spec for spec, _ in inputs] + [vmem_spec] * len(carried)
    arrays = []
    for spec, array in inputs:
        if spec is hbm_spec:
            array = pltpu.with_memory_space_constraint(array, pltpu.HBM)
        elif spec is vmem_spec:
            array = pltpu.with_memory_space_constraint(array, pltpu.VMEM)
        arrays.append(array)
    arrays += [pltpu.with_memory_space_constraint(a, pltpu.VMEM) for a in carried]
    out_specs = [spec for spec, _ in outs] + [vmem_spec] * len(carried)
    out_shape = [shape for _, shape in outs] + [pltpu.VMEM(a.shape, a.dtype) for a in carried]
    return pl.pallas_call(
        kernel,
        in_specs=specs,
        out_specs=out_specs,
        out_shape=out_shape,
        scratch_shapes=list(scratch),
        input_output_aliases={len(inputs) + n: len(outs) + n for n in range(len(carried))},
        compiler_params=pltpu.CompilerParams(vmem_limit_bytes=limit * 2**20),
        cost_estimate=work,
        name=name,
    )(*arrays)


def shift_up(x, axis):
    return lax.ppermute(x, axis, [(i, i + 1) for i in range(lax.axis_size(axis) - 1)])


def exchange(x, axis, mask):
    return lax.ppermute(x, axis, [(i, i ^ mask) for i in range(lax.axis_size(axis))])


def per_device(electric_x, electric_z, magnetic_x, magnetic_y, magnetic_z, material, perm_table):
    xs, ys, zs = material.shape
    chunks = xs // rows
    cells = xs * ys * zs
    V, H = pltpu.VMEM, pltpu.HBM
    fields = (electric_x, electric_z, magnetic_x, magnetic_y, magnetic_z)
    block = (2 * chunks, 5, 2 * rows, lane)

    y_t, y_drive, y_reduced, x_t, x_drive, x_reduced, yt_edge, my_edge, xt_edge, mx_edge = call(
        forward_kernel,
        "forward",
        [(hbm_spec, a) for a in (perm_table, material) + fields],
        [
            (vmem_spec, V((ys, xs, zs), f32)),
            (vmem_spec, V((ys, xs, zs), f32)),
            (vmem_spec, V(block, f32)),
            (hbm_spec, H((xs, ys, zs), f32)),
            (hbm_spec, H((xs, ys, zs), f32)),
            (vmem_spec, V((5, ys, zs), f32)),
            (vmem_spec, V((ys, xs, lane), f32)),
            (vmem_spec, V((rows, lane), f32)),
            (vmem_spec, V((xs, 1, zs), f32)),
            (vmem_spec, V((xs, zs), f32)),
        ],
        scratch=[pltpu.SMEM(perm_table.shape, f32), V((xs, ys, zs), jnp.int32)]
        + [V((xs, ys, zs), f32)] * 7
        + [V((zs // lane, rows * ys, lane), f32)] * 3
        + [V((rows * ys, lane), f32), V((5, ys, zs), f32), V((ys, zs), f32)]
        + [pltpu.SemaphoreType.DMA, pltpu.SemaphoreType.DMA((6, chunks)), pltpu.SemaphoreType.DMA((2, chunks))],
        limit=24,
        work=cost(cells, 60, 10),
    )

    edge_z = shift_up(my_edge, "gz")
    edge_y = shift_up(mx_edge, "gy")
    y_reduced, y_drive = pl.pallas_call(
        y_edge_kernel,
        in_specs=[vmem_spec] * 4,
        out_specs=[vmem_spec] * 2,
        out_shape=[H(block, f32), V((ys, xs, zs), f32)],
        input_output_aliases={3: 1},
        compiler_params=pltpu.CompilerParams(vmem_limit_bytes=8 * 2**20),
        cost_estimate=cost(cells // 4, 10, 3),
        name="y_edge",
    )(*(pltpu.with_memory_space_constraint(a, V) for a in (edge_z, yt_edge, y_reduced, y_drive)))
    y_reduced, edge_y = lax.optimization_barrier((y_reduced, edge_y))
    y_blocks = lax.all_to_all(y_reduced, "gy", 0, 0, tiled=True)

    x_reduced, kept = call(
        x_edge_kernel,
        "x_edge",
        [(vmem_spec, a) for a in (edge_y, xt_edge, x_reduced)],
        [(vmem_spec, V((5, ys, zs), f32)), (vmem_spec, V((kept_count, ys, zs), f32))],
        limit=8,
        work=cost(cells // ys, 10, 3),
    )

    (y_ends,) = pl.pallas_call(
        y_reduced_kernel,
        in_specs=[vmem_spec],
        out_specs=[vmem_spec],
        out_shape=[H((2 * chunks, 2, 2 * rows, lane), f32)],
        compiler_params=pltpu.CompilerParams(vmem_limit_bytes=8 * 2**20),
        cost_estimate=cost(y_blocks.size // 5, 20, 7),
        name="y_reduced",
    )(y_blocks)

    own = x_reduced
    for level, mask in enumerate((1, 3, 4)):
        other = exchange(own, "gx", mask)
        if level == 1:
            other, y_ends = lax.optimization_barrier((other, y_ends))
        kernel = functools.partial(merge_kernel if level < 2 else last_merge_kernel, level)

        def body(own_ref, other_ref, kept_in, *refs, kernel=kernel):
            merged_ref, kept_ref = refs[2], refs[3]
            kernel(own_ref, other_ref, kept_in, merged_ref, kept_ref)

        own, kept, y_t, y_drive = call(
            body,
            "x_merge",
            [(vmem_spec, own), (vmem_spec, other)],
            [(vmem_spec, V((5 if level < 2 else 2, ys, zs), f32))],
            carried=(kept, y_t, y_drive),
            limit=8,
            work=cost(own.size, 10, 3),
        )
    side_other = exchange(own, "gx", 12)
    y_ends = lax.all_to_all(y_ends, "gy", 0, 0, tiled=True)

    electric_x_half, x_t, x_drive = call(
        y_back_kernel,
        "y_back",
        [(vmem_spec, a) for a in (y_t, y_drive, y_ends)] + [(hbm_spec, a) for a in (x_t, x_drive)],
        [(hbm_spec, H((xs, ys, zs), f32))] + [(vmem_spec, V((xs, ys, zs), f32))] * 2,
        scratch=[V((zs // lane, rows * ys, lane), f32), V((xs, ys, zs), f32)]
        + [pltpu.SemaphoreType.DMA((chunks,)), pltpu.SemaphoreType.DMA((2,))],
        work=cost(cells, 5, 3),
    )
    (electric_z_half,) = call(
        x_back_kernel,
        "x_back",
        [(vmem_spec, a) for a in (x_t, x_drive, kept, own, side_other)],
        [(vmem_spec, H((xs, ys, zs), f32))],
        work=cost(cells, 5, 3),
    )
    return (electric_x_half, electric_z_half)


def solution(mesh):
    field = P("gx", "gy", "gz")
    return jax.shard_map(
        per_device,
        mesh=mesh,
        in_specs=(field,) * 6 + (P(),),
        out_specs=(field, field),
        check_vma=False,
    )
```

```python
import functools

import jax
import jax.numpy as jnp
from jax import lax
from jax.experimental import pallas as pl
from jax.experimental.pallas import tpu as pltpu
from jax.sharding import PartitionSpec as P

ground_scale = 1.0 / 1600.0
drive_scale = 1.0 / 40.0
lane = 128
rows = 8
f32 = jnp.float32
vmem_spec = pl.BlockSpec(memory_space=pltpu.VMEM)
any_spec = pl.BlockSpec(memory_space=pl.ANY)
hbm_spec = pl.BlockSpec(memory_space=pltpu.HBM)


def inverse(x):
    return pltpu.reciprocal(x, approx=True)


def eliminate(state, ground, drive):
    link, left, here, left_drive, here_drive = state
    t = inverse(link + here + 1.0)
    next_link = link * t
    return (
        next_link,
        left + next_link * here,
        ground + here * t,
        left_drive + next_link * here_drive,
        drive + here_drive * t,
    ), t


def close_block(state, rim):
    link, left, here, left_drive, here_drive = state
    return (
        link,
        left,
        here,
        left_drive + link * rim,
        here_drive - (link + here + 1.0) * rim,
    )


def forward_kernel(
    table_hbm, material_hbm, ex_hbm, ez_hbm, mx_hbm, my_hbm, mz_hbm,
    yt_ref, ydrive_ref, yreduced_ref, xt_hbm, xdrive_hbm, xreduced_ref,
    yt_edge_ref, my_edge_ref, xt_edge_ref, mx_edge_ref,
    table_s, material_s, ex_s, ez_s, mx_s, my_s, mz_s, xt_s, xjs_s, ground_s, ydrive_s, xdrive_s, turn_s,
    state_s, last_my_s, table_sem, sems, out_sems,
):
    xs, ys, zs = material_s.shape
    tiles = zs // lane
    chunks = xs // rows
    flat = (rows * ys, lane)
    cube = (rows, ys, lane)
    arrays = (
        (material_hbm, material_s), (my_hbm, my_s), (mz_hbm, mz_s),
        (ex_hbm, ex_s), (ez_hbm, ez_s), (mx_hbm, mx_s),
    )

    def chunk_copies(c):
        part = pl.ds(pl.multiple_of(c * rows, rows), rows)
        return [
            pltpu.make_async_copy(source.at[part], target.at[part], sems.at[a, c])
            for a, (source, target) in enumerate(arrays)
        ]

    def chunk_stores(c):
        part = pl.ds(pl.multiple_of(c * rows, rows), rows)
        return [
            pltpu.make_async_copy(source.at[part], target.at[part], out_sems.at[a, c])
            for a, (source, target) in enumerate(((xt_s, xt_hbm), (xjs_s, xdrive_hbm)))
        ]

    table_copy = pltpu.make_async_copy(table_hbm, table_s, table_sem)
    table_copy.start()
    for c in range(chunks):
        for copy in chunk_copies(c):
            copy.start()
    lanes = lax.broadcasted_iota(jnp.int32, flat, 1)
    first_lane = lanes == 0
    first_y = lax.broadcasted_iota(jnp.int32, cube, 1) == 0
    edge_lanes = lax.broadcasted_iota(jnp.int32, (rows, lane), 1)
    my_edge_ref[...] = jnp.zeros_like(my_edge_ref)
    state_s[...] = jnp.zeros_like(state_s)
    last_my_s[...] = jnp.zeros_like(last_my_s)
    table_copy.wait()
    table = jnp.zeros((1, lane), f32)
    for m in range(table_s.shape[0]):
        table = jnp.where(lax.broadcasted_iota(jnp.int32, (1, lane), 1) == m, table_s[m], table)
    table = table * ground_scale

    def chunk(c, _):
        for copy in chunk_copies(c):
            copy.wait()
        part = pl.ds(pl.multiple_of(c * rows, rows), rows)
        before = jnp.zeros(flat, f32)
        for k in range(tiles):
            cut = pl.ds(k * lane, lane)
            ground = jnp.take_along_axis(
                jnp.broadcast_to(table, flat), material_s[part, :, cut].reshape(flat), axis=1, mode="promise_in_bounds"
            )
            my = my_s[part, :, cut]
            rolled = pltpu.roll(my.reshape(flat), 1, 1)
            my_step = my.reshape(flat) - jnp.where(first_lane, before, rolled)
            before = rolled
            mz = mz_s[part, :, cut]
            mz_step = (mz - jnp.where(first_y, 0.0, pltpu.roll(mz, 1, 1))).reshape(flat)
            mx = mx_s[part, :, cut]
            mx_step = (mx - jnp.where(first_y, 0.0, pltpu.roll(mx, 1, 1))).reshape(flat)
            my_up = (my - jnp.concatenate([last_my_s[:, cut][None], my[:-1]], axis=0)).reshape(flat)
            last_my_s[:, cut] = my[rows - 1]
            ground_s[k] = ground
            ydrive_s[k] = ground * ex_s[part, :, cut].reshape(flat) + drive_scale * (mz_step - my_step)
            xdrive_s[k] = ground * ez_s[part, :, cut].reshape(flat) + drive_scale * (my_up - mx_step)
            mx_edge_ref[part, cut] = mx_s[part, ys - 1, cut]
            if k == tiles - 1:
                turn_s[...] = my.reshape(flat)

        states = [tuple(state_s[v, :, pl.ds(k * lane, lane)] for v in range(5)) for k in range(tiles)]
        for i in range(rows):
            line = pl.ds(i * ys, ys)
            for k in range(tiles):
                cut = pl.ds(k * lane, lane)
                state, t = eliminate(states[k], ground_s[k, line, :], xdrive_s[k, line, :])
                if i == 0:
                    state = (jnp.where(c == 0, 1.0, state[0]),) + state[1:]
                states[k] = state
                xt_s[c * rows + i, :, cut] = t
                js = state[4]
                if i == rows - 1:
                    js = jnp.where(c == chunks - 1, drive_scale * last_my_s[:, cut], js)
                xjs_s[c * rows + i, :, cut] = js
                xt_edge_ref[c * rows + i, :, cut] = t[0:1]
        for k in range(tiles):
            for v in range(5):
                state_s[v, :, pl.ds(k * lane, lane)] = states[k][v]
        for copy in chunk_stores(c):
            copy.start()

        for first in range(0, tiles, 2):
            pair = (first, first + 1)
            states = [None, None]
            for j in range(ys):
                pick = pl.ds(j, rows, stride=ys)
                for n, k in enumerate(pair):
                    cut = pl.ds(k * lane, lane)
                    ground = ground_s[k, pick, :]
                    drive = ydrive_s[k, pick, :]
                    if j == 0:
                        zero = jnp.zeros_like(ground)
                        states[n] = (jnp.ones_like(ground), zero, ground, zero, drive)
                    else:
                        states[n], t = eliminate(states[n], ground, drive)
                        yt_ref[j - 1, part, cut] = t
                        if k == 0:
                            yt_edge_ref[j - 1, part, :] = t
                    if j < ys - 1:
                        ydrive_ref[j, part, cut] = states[n][4]
            for n, k in enumerate(pair):
                cut = pl.ds(k * lane, lane)
                rim = drive_scale * mz_s[part, ys - 1, cut]
                ydrive_ref[ys - 1, part, cut] = rim
                for v, value in enumerate(close_block(states[n], rim)):
                    yreduced_ref[2 * c + k // 2, v, pl.ds((k % 2) * rows, rows), :] = value
        packed = my_edge_ref[...]
        for j in range(ys):
            place = j * chunks + c
            turned = pltpu.roll(turn_s[pl.ds(j, rows, stride=ys), :], place + 1, 1)
            packed = jnp.where(edge_lanes == place, turned, packed)
        my_edge_ref[...] = packed
        return _

    lax.fori_loop(0, chunks, chunk, 0)
    rim = drive_scale * last_my_s[...]
    for v, value in enumerate(close_block(tuple(state_s[v] for v in range(5)), rim)):
        xreduced_ref[v] = value
    for c in range(chunks):
        for copy in chunk_stores(c):
            copy.wait()


def y_edge_kernel(edge_ref, t_ref, reduced_ref, drive_ref, reduced_out, drive_out):
    ys, xs, _ = t_ref.shape
    reduced_out[...] = reduced_ref[...]
    first_lane = lax.broadcasted_iota(jnp.int32, (rows, lane), 1) == 0
    first_lane = first_lane & (lax.axis_index("gz") == 1)
    for c in range(xs // rows):
        part = pl.ds(c * rows, rows)

        def rim(j, c=c):
            place = j * (xs // rows) + c
            turned = pltpu.roll(edge_ref[...], (lane - place) % lane, 1)
            return jnp.where(first_lane, drive_scale * turned, 0.0)

        here = rim(0)
        link = jnp.ones_like(here)
        left = jnp.zeros_like(here)
        for j in range(ys):
            if j > 0:
                t = t_ref[j - 1, part, :]
                link = link * t
                left = left + link * here
                here = rim(j) + here * t
            if j < ys - 1:
                drive_out[j, part, pl.ds(0, lane)] = drive_ref[j, part, pl.ds(0, lane)] + here
        reduced_out[2 * c, 3, pl.ds(0, rows), :] = reduced_ref[2 * c, 3, pl.ds(0, rows), :] + left
        reduced_out[2 * c, 4, pl.ds(0, rows), :] = reduced_ref[2 * c, 4, pl.ds(0, rows), :] + here


kept_count = 13


def x_edge_kernel(odd_ref, even_ref, t_ref, reduced_ref, reduced_out, kept_ref):
    xs = t_ref.shape[0]
    ys = reduced_ref.shape[1]
    row = pl.ds(0, 1)
    place = lax.axis_index("gy")
    scale_odd = jnp.where(place % 2 == 1, drive_scale, 0.0)
    scale_even = jnp.where((place % 2 == 0) & (place > 0), drive_scale, 0.0)
    edge = scale_odd * odd_ref[...] + scale_even * even_ref[...]
    here = edge[0:1]
    link = jnp.ones_like(here)
    left = jnp.zeros_like(here)
    kept_ref[11, row, :] = here
    for i in range(1, xs):
        t = t_ref[i]
        link = link * t
        left = left + link * here
        here = edge[i:i + 1] + here * t
        kept_ref[11 + i // ys, pl.ds(i % ys, 1), :] = here
    for v in range(5):
        reduced_out[v] = reduced_ref[v]
    reduced_out[3, row, :] = reduced_ref[3, row, :] + left
    reduced_out[4, row, :] = reduced_ref[4, row, :] + here


def y_reduced_kernel(blocks_ref, ends_ref):
    count = blocks_ref.shape[0]
    block = [[blocks_ref[b, v] for v in range(5)] for b in range(count)]
    here = block[0][2] + block[0][0]
    drive = block[0][4]
    kept = []
    for b in range(1, count):
        link, left, right, left_drive, right_drive = block[b]
        total = here + left
        t = inverse(total + link)
        pull = link * t
        push = drive + left_drive
        kept.append((pull, push * t))
        here = right + pull * total
        drive = right_drive + pull * push
    value = drive * inverse(here + 1.0)
    ends_ref[count - 1, 1] = value
    for b in range(count - 1, 0, -1):
        pull, push = kept[b - 1]
        value = push + pull * value
        ends_ref[b, 0] = value
        ends_ref[b - 1, 1] = value
    ends_ref[0, 0] = jnp.zeros_like(value)


def merge(low, own_ref, other_ref, kept_ref, slot):
    own = [own_ref[v] for v in range(5)]
    other = [other_ref[v] for v in range(5)]
    a = [jnp.where(low, p, q) for p, q in zip(own, other)]
    b = [jnp.where(low, q, p) for p, q in zip(own, other)]
    total = a[2] + b[1]
    t = inverse(total + a[0] + b[0])
    a_link, b_link = a[0] * t, b[0] * t
    push = a[4] + b[3]
    kept_ref[slot] = push * t
    kept_ref[slot + 1] = a_link
    kept_ref[slot + 2] = b_link
    return (
        a[0] * b_link,
        a[1] + a_link * total,
        b[2] + b_link * total,
        a[3] + a_link * push,
        b[4] + b_link * push,
    )


def is_low(level):
    return (lax.axis_index("gx") >> level) & 1 == 0


def merge_kernel(level, own_ref, other_ref, _, merged_ref, kept_ref):
    merged = merge(is_low(level), own_ref, other_ref, kept_ref, 3 * level)
    for v in range(5):
        merged_ref[v] = merged[v]


def last_merge_kernel(level, own_ref, other_ref, _, side_ref, kept_ref):
    link, left, right, left_drive, right_drive = merge(is_low(level), own_ref, other_ref, kept_ref, 3 * level)
    closed = inverse(right + link + 1.0)
    share = link * closed
    top = is_low(level + 1)
    side_ref[0] = jnp.where(top, right + link, left + share * (right + 1.0))
    side_ref[1] = jnp.where(top, right_drive, left_drive + share * right_drive)
    kept_ref[9] = closed * right_drive
    kept_ref[10] = share


def y_back_kernel(
    t_ref, drive_ref, ends_ref, xt_hbm, xdrive_hbm, out_hbm, xt_ref, xdrive_ref, turn_s, out_s, sems, load_sems
):
    loads = [
        pltpu.make_async_copy(xt_hbm, xt_ref, load_sems.at[0]),
        pltpu.make_async_copy(xdrive_hbm, xdrive_ref, load_sems.at[1]),
    ]
    for load in loads:
        load.start()
    ys, xs, zs = t_ref.shape
    copies = []
    for c in range(xs // rows):
        part = pl.ds(c * rows, rows)
        for k in range(zs // lane):
            cut = pl.ds(k * lane, lane)
            half = pl.ds((k % 2) * rows, rows)
            reach = ends_ref[2 * c + k // 2, 0, half, :]
            value = ends_ref[2 * c + k // 2, 1, half, :] + drive_ref[ys - 1, part, cut]
            parts = []
            for j in range(ys - 1):
                t = t_ref[j, part, cut]
                reach = reach * t
                parts.append((t, drive_ref[j, part, cut] * t + reach))
            turn_s[k, pl.ds(ys - 1, rows, stride=ys), :] = value
            for j in range(ys - 2, -1, -1):
                t, share = parts[j]
                value = share + t * value
                turn_s[k, pl.ds(j, rows, stride=ys), :] = value
            out_s[part, :, cut] = turn_s[k].reshape(rows, ys, lane)
        copies.append(pltpu.make_async_copy(out_s.at[part], out_hbm.at[part], sems.at[c]))
        copies[-1].start()
    for copy in copies + loads:
        copy.wait()


def x_back_kernel(t_ref, drive_ref, kept_ref, side_ref, other_ref, out_ref):
    xs, ys, zs = t_ref.shape
    top = is_low(3)
    middle = (side_ref[1] + other_ref[1]) * inverse(side_ref[0] + other_ref[0])
    before = jnp.where(top, 0.0, middle)
    here = jnp.where(top, middle, kept_ref[9] + kept_ref[10] * middle)
    for level in (2, 1, 0):
        low = is_low(level)
        middle = kept_ref[3 * level] + kept_ref[3 * level + 1] * before + kept_ref[3 * level + 2] * here
        before, here = jnp.where(low, before, middle), jnp.where(low, middle, here)
    first_y = lax.broadcasted_iota(jnp.int32, (ys, zs), 0) == 0
    reach = before
    for i in range(xs - 1):
        t = t_ref[i + 1]
        reach = reach * t
        edge = jnp.where(first_y, kept_ref[11 + i // ys, pl.ds(i % ys, 1), :], 0.0)
        out_ref[i] = (drive_ref[i] + edge) * t + reach
    value = here + drive_ref[xs - 1]
    out_ref[xs - 1] = value
    for i in range(xs - 2, -1, -1):
        value = out_ref[i] + t_ref[i + 1] * value
        out_ref[i] = value


def cost(elements, ops, arrays):
    return pl.CostEstimate(flops=elements * ops, bytes_accessed=elements * 4 * arrays, transcendentals=0)


def call(kernel, name, inputs, outs, carried=(), limit=16, work=None, scratch=()):
    specs = [spec for spec, _ in inputs] + [vmem_spec] * len(carried)
    arrays = []
    for spec, array in inputs:
        if spec is hbm_spec:
            array = pltpu.with_memory_space_constraint(array, pltpu.HBM)
        elif spec is vmem_spec:
            array = pltpu.with_memory_space_constraint(array, pltpu.VMEM)
        arrays.append(array)
    arrays += [pltpu.with_memory_space_constraint(a, pltpu.VMEM) for a in carried]
    out_specs = [spec for spec, _ in outs] + [vmem_spec] * len(carried)
    out_shape = [shape for _, shape in outs] + [pltpu.VMEM(a.shape, a.dtype) for a in carried]
    return pl.pallas_call(
        kernel,
        in_specs=specs,
        out_specs=out_specs,
        out_shape=out_shape,
        scratch_shapes=list(scratch),
        input_output_aliases={len(inputs) + n: len(outs) + n for n in range(len(carried))},
        compiler_params=pltpu.CompilerParams(vmem_limit_bytes=limit * 2**20),
        cost_estimate=work,
        name=name,
    )(*arrays)


def exchange(x, axis, mask):
    return lax.ppermute(x, axis, [(i, i ^ mask) for i in range(lax.axis_size(axis))])


def per_device(electric_x, electric_z, magnetic_x, magnetic_y, magnetic_z, material, perm_table):
    xs, ys, zs = material.shape
    chunks = xs // rows
    cells = xs * ys * zs
    V, H = pltpu.VMEM, pltpu.HBM
    fields = (electric_x, electric_z, magnetic_x, magnetic_y, magnetic_z)
    block = (2 * chunks, 5, 2 * rows, lane)

    y_t, y_drive, y_reduced, x_t, x_drive, x_reduced, yt_edge, my_edge, xt_edge, mx_edge = call(
        forward_kernel,
        "forward",
        [(hbm_spec, a) for a in (perm_table, material) + fields],
        [
            (vmem_spec, V((ys, xs, zs), f32)),
            (vmem_spec, V((ys, xs, zs), f32)),
            (vmem_spec, V(block, f32)),
            (hbm_spec, H((xs, ys, zs), f32)),
            (hbm_spec, H((xs, ys, zs), f32)),
            (vmem_spec, V((5, ys, zs), f32)),
            (vmem_spec, V((ys, xs, lane), f32)),
            (vmem_spec, V((rows, lane), f32)),
            (vmem_spec, V((xs, 1, zs), f32)),
            (vmem_spec, V((xs, zs), f32)),
        ],
        scratch=[pltpu.SMEM(perm_table.shape, f32), V((xs, ys, zs), jnp.int32)]
        + [V((xs, ys, zs), f32)] * 7
        + [V((zs // lane, rows * ys, lane), f32)] * 3
        + [V((rows * ys, lane), f32), V((5, ys, zs), f32), V((ys, zs), f32)]
        + [pltpu.SemaphoreType.DMA, pltpu.SemaphoreType.DMA((6, chunks)), pltpu.SemaphoreType.DMA((2, chunks))],
        limit=24,
        work=cost(cells, 60, 10),
    )

    edge_z = exchange(my_edge, "gz", 1)
    edge_odd = exchange(mx_edge, "gy", 1)
    edge_even = lax.ppermute(mx_edge, "gy", [(i, (i + (1 if i % 2 else -1)) % lax.axis_size("gy")) for i in range(lax.axis_size("gy"))])
    y_reduced, y_drive = pl.pallas_call(
        y_edge_kernel,
        in_specs=[vmem_spec] * 4,
        out_specs=[vmem_spec] * 2,
        out_shape=[H(block, f32), V((ys, xs, zs), f32)],
        input_output_aliases={3: 1},
        compiler_params=pltpu.CompilerParams(vmem_limit_bytes=8 * 2**20),
        cost_estimate=cost(cells // 4, 10, 3),
        name="y_edge",
    )(*(pltpu.with_memory_space_constraint(a, V) for a in (edge_z, yt_edge, y_reduced, y_drive)))
    y_reduced, edge_odd, edge_even = lax.optimization_barrier((y_reduced, edge_odd, edge_even))
    y_blocks = lax.all_to_all(y_reduced, "gy", 0, 0, tiled=True)

    x_reduced, kept = call(
        x_edge_kernel,
        "x_edge",
        [(vmem_spec, a) for a in (edge_odd, edge_even, xt_edge, x_reduced)],
        [(vmem_spec, V((5, ys, zs), f32)), (vmem_spec, V((kept_count, ys, zs), f32))],
        limit=8,
        work=cost(cells // ys, 10, 3),
    )

    (y_ends,) = pl.pallas_call(
        y_reduced_kernel,
        in_specs=[vmem_spec],
        out_specs=[vmem_spec],
        out_shape=[H((2 * chunks, 2, 2 * rows, lane), f32)],
        compiler_params=pltpu.CompilerParams(vmem_limit_bytes=8 * 2**20),
        cost_estimate=cost(y_blocks.size // 5, 20, 7),
        name="y_reduced",
    )(y_blocks)

    own = x_reduced
    for level, mask in enumerate((1, 3, 4)):
        other = exchange(own, "gx", mask)
        kernel = functools.partial(merge_kernel if level < 2 else last_merge_kernel, level)

        def body(own_ref, other_ref, *refs, kernel=kernel):
            merged_ref, kept_ref = refs[-4:-2]
            kernel(own_ref, other_ref, None, merged_ref, kept_ref)

        own, kept, y_t, y_drive = call(
            body,
            "x_merge",
            [(vmem_spec, own), (vmem_spec, other)] + ([(any_spec, y_ends)] if level == 1 else []),
            [(vmem_spec, V((5 if level < 2 else 2, ys, zs), f32))],
            carried=(kept, y_t, y_drive),
            limit=8,
            work=cost(own.size, 10, 3),
        )
    side_other = exchange(own, "gx", 12)
    y_ends = lax.all_to_all(y_ends, "gy", 0, 0, tiled=True)

    electric_x_half, x_t, x_drive = call(
        y_back_kernel,
        "y_back",
        [(vmem_spec, a) for a in (y_t, y_drive, y_ends)] + [(hbm_spec, a) for a in (x_t, x_drive)],
        [(hbm_spec, H((xs, ys, zs), f32))] + [(vmem_spec, V((xs, ys, zs), f32))] * 2,
        scratch=[V((zs // lane, rows * ys, lane), f32), V((xs, ys, zs), f32)]
        + [pltpu.SemaphoreType.DMA((chunks,)), pltpu.SemaphoreType.DMA((2,))],
        work=cost(cells, 5, 3),
    )
    (electric_z_half,) = call(
        x_back_kernel,
        "x_back",
        [(vmem_spec, a) for a in (x_t, x_drive, kept, own, side_other)],
        [(vmem_spec, H((xs, ys, zs), f32))],
        work=cost(cells, 5, 3),
    )
    return (electric_x_half, electric_z_half)


def solution(mesh):
    field = P("gx", "gy", "gz")
    return jax.shard_map(
        per_device,
        mesh=mesh,
        in_specs=(field,) * 6 + (P(),),
        out_specs=(field, field),
        check_vma=False,
    )
```

```python
import functools

import jax
import jax.numpy as jnp
from jax import lax
from jax.experimental import pallas as pl
from jax.experimental.pallas import tpu as pltpu
from jax.sharding import PartitionSpec as P

ground_scale = 1.0 / 1600.0
drive_scale = 1.0 / 40.0
lane = 128
rows = 8
f32 = jnp.float32
vmem_spec = pl.BlockSpec(memory_space=pltpu.VMEM)
any_spec = pl.BlockSpec(memory_space=pl.ANY)
hbm_spec = pl.BlockSpec(memory_space=pltpu.HBM)


def inverse(x):
    return pltpu.reciprocal(x, approx=True)


def eliminate(state, ground, drive):
    link, left, here, left_drive, here_drive = state
    t = inverse(link + here + 1.0)
    next_link = link * t
    return (
        next_link,
        left + next_link * here,
        ground + here * t,
        left_drive + next_link * here_drive,
        drive + here_drive * t,
    ), t


def close_block(state, rim):
    link, left, here, left_drive, here_drive = state
    return (
        link,
        left,
        here,
        left_drive + link * rim,
        here_drive - (link + here + 1.0) * rim,
    )


def forward_kernel(
    table_hbm, material_hbm, ex_hbm, ez_hbm, mx_hbm, my_hbm, mz_hbm,
    yt_ref, ydrive_ref, yreduced_ref, xt_ref, xdrive_ref, xreduced_ref,
    yt_edge_ref, my_edge_ref, xt_edge_ref, mx_edge_ref,
    table_s, material_s, ex_s, ez_s, mx_s, my_s, mz_s, ground_s, yground_s, ydrive_s, xdrive_s, turn_s,
    state_s, last_my_s, table_sem, sems,
):
    xs, ys, zs = material_s.shape
    tiles = zs // lane
    chunks = xs // rows
    flat = (rows * ys, lane)
    cube = (rows, ys, lane)
    arrays = (
        (material_hbm, material_s), (my_hbm, my_s), (mz_hbm, mz_s),
        (ex_hbm, ex_s), (ez_hbm, ez_s), (mx_hbm, mx_s),
    )

    def chunk_copies(c):
        part = pl.ds(pl.multiple_of(c * rows, rows), rows)
        return [
            pltpu.make_async_copy(source.at[part], target.at[part], sems.at[a, c])
            for a, (source, target) in enumerate(arrays)
        ]

    table_copy = pltpu.make_async_copy(table_hbm, table_s, table_sem)
    table_copy.start()
    for c in range(chunks):
        for copy in chunk_copies(c):
            copy.start()
    lanes = lax.broadcasted_iota(jnp.int32, flat, 1)
    first_lane = lanes == 0
    first_y = lax.broadcasted_iota(jnp.int32, cube, 1) == 0
    edge_lanes = lax.broadcasted_iota(jnp.int32, (rows, lane), 1)
    my_edge_ref[...] = jnp.zeros_like(my_edge_ref)
    state_s[...] = jnp.zeros_like(state_s)
    last_my_s[...] = jnp.zeros_like(last_my_s)
    table_copy.wait()
    table = jnp.zeros((1, lane), f32)
    for m in range(table_s.shape[0]):
        table = jnp.where(lax.broadcasted_iota(jnp.int32, (1, lane), 1) == m, table_s[m], table)
    table = table * ground_scale

    def chunk(c, _):
        for copy in chunk_copies(c):
            copy.wait()
        part = pl.ds(pl.multiple_of(c * rows, rows), rows)
        before = jnp.zeros(flat, f32)
        for k in range(tiles):
            cut = pl.ds(k * lane, lane)
            ground = jnp.take_along_axis(
                jnp.broadcast_to(table, flat), material_s[part, :, cut].reshape(flat), axis=1, mode="promise_in_bounds"
            )
            my = my_s[part, :, cut]
            rolled = pltpu.roll(my.reshape(flat), 1, 1)
            my_step = my.reshape(flat) - jnp.where(first_lane, before, rolled)
            before = rolled
            mz = mz_s[part, :, cut]
            mz_step = (mz - jnp.where(first_y, 0.0, pltpu.roll(mz, 1, 1))).reshape(flat)
            mx = mx_s[part, :, cut]
            mx_step = (mx - jnp.where(first_y, 0.0, pltpu.roll(mx, 1, 1))).reshape(flat)
            my_up = (my - jnp.concatenate([last_my_s[:, cut][None], my[:-1]], axis=0)).reshape(flat)
            last_my_s[:, cut] = my[rows - 1]
            ground_s[k] = ground
            ydrive = ground * ex_s[part, :, cut].reshape(flat) + drive_scale * (mz_step - my_step)
            for i in range(rows):
                for h in range(0, ys, rows):
                    turned = pl.ds(h * rows + i, rows, stride=rows)
                    natural = slice(i * ys + h, i * ys + h + rows)
                    yground_s[k, turned, :] = ground[natural]
                    ydrive_s[k, turned, :] = ydrive[natural]
            xdrive_s[k] = ground * ez_s[part, :, cut].reshape(flat) + drive_scale * (my_up - mx_step)
            mx_edge_ref[part, cut] = mx_s[part, ys - 1, cut]
            if k == tiles - 1:
                turn_s[...] = my.reshape(flat)

        states = [tuple(state_s[v, :, pl.ds(k * lane, lane)] for v in range(5)) for k in range(tiles)]
        for i in range(rows):
            line = pl.ds(i * ys, ys)
            for k in range(tiles):
                cut = pl.ds(k * lane, lane)
                state, t = eliminate(states[k], ground_s[k, line, :], xdrive_s[k, line, :])
                if i == 0:
                    state = (jnp.where(c == 0, 1.0, state[0]),) + state[1:]
                states[k] = state
                xt_ref[c * rows + i, :, cut] = t
                js = state[4]
                if i == rows - 1:
                    js = jnp.where(c == chunks - 1, drive_scale * last_my_s[:, cut], js)
                xdrive_ref[c * rows + i, :, cut] = js
                xt_edge_ref[c * rows + i, :, cut] = t[0:1]
        for k in range(tiles):
            for v in range(5):
                state_s[v, :, pl.ds(k * lane, lane)] = states[k][v]

        for first in range(0, tiles, 2):
            pair = (first, first + 1)
            states = [None, None]
            for j in range(ys):
                pick = pl.ds(j * rows, rows)
                for n, k in enumerate(pair):
                    cut = pl.ds(k * lane, lane)
                    ground = yground_s[k, pick, :]
                    drive = ydrive_s[k, pick, :]
                    if j == 0:
                        zero = jnp.zeros_like(ground)
                        states[n] = (jnp.ones_like(ground), zero, ground, zero, drive)
                    else:
                        states[n], t = eliminate(states[n], ground, drive)
                        yt_ref[j - 1, part, cut] = t
                        if k == 0:
                            yt_edge_ref[j - 1, part, :] = t
                    if j < ys - 1:
                        ydrive_ref[j, part, cut] = states[n][4]
            for n, k in enumerate(pair):
                cut = pl.ds(k * lane, lane)
                rim = drive_scale * mz_s[part, ys - 1, cut]
                ydrive_ref[ys - 1, part, cut] = rim
                for v, value in enumerate(close_block(states[n], rim)):
                    yreduced_ref[2 * c + k // 2, v, pl.ds((k % 2) * rows, rows), :] = value
        packed = my_edge_ref[...]
        for j in range(ys):
            place = j * chunks + c
            turned = pltpu.roll(turn_s[pl.ds(j, rows, stride=ys), :], place + 1, 1)
            packed = jnp.where(edge_lanes == place, turned, packed)
        my_edge_ref[...] = packed
        return _

    lax.fori_loop(0, chunks, chunk, 0)
    rim = drive_scale * last_my_s[...]
    for v, value in enumerate(close_block(tuple(state_s[v] for v in range(5)), rim)):
        xreduced_ref[v] = value


def y_edge_kernel(edge_ref, t_ref, reduced_ref, drive_ref, reduced_out, drive_out):
    ys, xs, _ = t_ref.shape
    reduced_out[...] = reduced_ref[...]
    first_lane = lax.broadcasted_iota(jnp.int32, (rows, lane), 1) == 0
    first_lane = first_lane & (lax.axis_index("gz") == 1)
    for c in range(xs // rows):
        part = pl.ds(c * rows, rows)

        def rim(j, c=c):
            place = j * (xs // rows) + c
            turned = pltpu.roll(edge_ref[...], (lane - place) % lane, 1)
            return jnp.where(first_lane, drive_scale * turned, 0.0)

        here = rim(0)
        link = jnp.ones_like(here)
        left = jnp.zeros_like(here)
        for j in range(ys):
            if j > 0:
                t = t_ref[j - 1, part, :]
                link = link * t
                left = left + link * here
                here = rim(j) + here * t
            if j < ys - 1:
                drive_out[j, part, pl.ds(0, lane)] = drive_ref[j, part, pl.ds(0, lane)] + here
        reduced_out[2 * c, 3, pl.ds(0, rows), :] = reduced_ref[2 * c, 3, pl.ds(0, rows), :] + left
        reduced_out[2 * c, 4, pl.ds(0, rows), :] = reduced_ref[2 * c, 4, pl.ds(0, rows), :] + here


kept_count = 13


def x_edge_kernel(edge_ref, t_ref, reduced_ref, reduced_out, kept_ref):
    xs = t_ref.shape[0]
    ys = reduced_ref.shape[1]
    row = pl.ds(0, 1)
    edge = jnp.where(lax.axis_index("gy") > 0, drive_scale, 0.0) * edge_ref[...]
    here = edge[0:1]
    link = jnp.ones_like(here)
    left = jnp.zeros_like(here)
    kept_ref[11, row, :] = here
    for i in range(1, xs):
        t = t_ref[i]
        link = link * t
        left = left + link * here
        here = edge[i:i + 1] + here * t
        kept_ref[11 + i // ys, pl.ds(i % ys, 1), :] = here
    for v in range(5):
        reduced_out[v] = reduced_ref[v]
    reduced_out[3, row, :] = reduced_ref[3, row, :] + left
    reduced_out[4, row, :] = reduced_ref[4, row, :] + here


def y_reduced_kernel(blocks_ref, ends_ref):
    count = blocks_ref.shape[0]
    block = [[blocks_ref[b, v] for v in range(5)] for b in range(count)]
    here = block[0][2] + block[0][0]
    drive = block[0][4]
    kept = []
    for b in range(1, count):
        link, left, right, left_drive, right_drive = block[b]
        total = here + left
        t = inverse(total + link)
        pull = link * t
        push = drive + left_drive
        kept.append((pull, push * t))
        here = right + pull * total
        drive = right_drive + pull * push
    value = drive * inverse(here + 1.0)
    ends_ref[count - 1, 1] = value
    for b in range(count - 1, 0, -1):
        pull, push = kept[b - 1]
        value = push + pull * value
        ends_ref[b, 0] = value
        ends_ref[b - 1, 1] = value
    ends_ref[0, 0] = jnp.zeros_like(value)


def merge(low, own_ref, other_ref, kept_ref, slot):
    own = [own_ref[v] for v in range(5)]
    other = [other_ref[v] for v in range(5)]
    a = [jnp.where(low, p, q) for p, q in zip(own, other)]
    b = [jnp.where(low, q, p) for p, q in zip(own, other)]
    total = a[2] + b[1]
    t = inverse(total + a[0] + b[0])
    a_link, b_link = a[0] * t, b[0] * t
    push = a[4] + b[3]
    kept_ref[slot] = push * t
    kept_ref[slot + 1] = a_link
    kept_ref[slot + 2] = b_link
    return (
        a[0] * b_link,
        a[1] + a_link * total,
        b[2] + b_link * total,
        a[3] + a_link * push,
        b[4] + b_link * push,
    )


def is_low(level):
    return (lax.axis_index("gx") >> level) & 1 == 0


def merge_kernel(level, own_ref, other_ref, _, merged_ref, kept_ref):
    merged = merge(is_low(level), own_ref, other_ref, kept_ref, 3 * level)
    for v in range(5):
        merged_ref[v] = merged[v]


def last_merge_kernel(level, own_ref, other_ref, _, side_ref, kept_ref):
    link, left, right, left_drive, right_drive = merge(is_low(level), own_ref, other_ref, kept_ref, 3 * level)
    closed = inverse(right + link + 1.0)
    share = link * closed
    top = is_low(level + 1)
    side_ref[0] = jnp.where(top, right + link, left + share * (right + 1.0))
    side_ref[1] = jnp.where(top, right_drive, left_drive + share * right_drive)
    kept_ref[9] = closed * right_drive
    kept_ref[10] = share


def y_back_kernel(
    t_ref, drive_ref, ends_ref, xt_hbm, xdrive_hbm, out_hbm, xt_ref, xdrive_ref, turn_s, out_s, sems, load_sems
):
    loads = [
        pltpu.make_async_copy(xt_hbm, xt_ref, load_sems.at[0]),
        pltpu.make_async_copy(xdrive_hbm, xdrive_ref, load_sems.at[1]),
    ]
    for load in loads:
        load.start()
    ys, xs, zs = t_ref.shape
    copies = []
    for c in range(xs // rows):
        part = pl.ds(c * rows, rows)
        for k in range(zs // lane):
            cut = pl.ds(k * lane, lane)
            half = pl.ds((k % 2) * rows, rows)
            reach = ends_ref[2 * c + k // 2, 0, half, :]
            value = ends_ref[2 * c + k // 2, 1, half, :] + drive_ref[ys - 1, part, cut]
            parts = []
            for j in range(ys - 1):
                t = t_ref[j, part, cut]
                reach = reach * t
                parts.append((t, drive_ref[j, part, cut] * t + reach))
            turn_s[k, pl.ds(ys - 1, rows, stride=ys), :] = value
            for j in range(ys - 2, -1, -1):
                t, share = parts[j]
                value = share + t * value
                turn_s[k, pl.ds(j, rows, stride=ys), :] = value
            out_s[part, :, cut] = turn_s[k].reshape(rows, ys, lane)
        copies.append(pltpu.make_async_copy(out_s.at[part], out_hbm.at[part], sems.at[c]))
        copies[-1].start()
    for copy in copies + loads:
        copy.wait()


def x_back_kernel(t_ref, drive_ref, kept_ref, side_ref, other_ref, out_ref):
    xs, ys, zs = t_ref.shape
    top = is_low(3)
    middle = (side_ref[1] + other_ref[1]) * inverse(side_ref[0] + other_ref[0])
    before = jnp.where(top, 0.0, middle)
    here = jnp.where(top, middle, kept_ref[9] + kept_ref[10] * middle)
    for level in (2, 1, 0):
        low = is_low(level)
        middle = kept_ref[3 * level] + kept_ref[3 * level + 1] * before + kept_ref[3 * level + 2] * here
        before, here = jnp.where(low, before, middle), jnp.where(low, middle, here)
    first_y = lax.broadcasted_iota(jnp.int32, (ys, zs), 0) == 0
    reach = before
    for i in range(xs - 1):
        t = t_ref[i + 1]
        reach = reach * t
        edge = jnp.where(first_y, kept_ref[11 + i // ys, pl.ds(i % ys, 1), :], 0.0)
        out_ref[i] = (drive_ref[i] + edge) * t + reach
    value = here + drive_ref[xs - 1]
    out_ref[xs - 1] = value
    for i in range(xs - 2, -1, -1):
        value = out_ref[i] + t_ref[i + 1] * value
        out_ref[i] = value


def store_kernel(t_ref, drive_ref, t_hbm, drive_hbm, sems):
    copies = [
        pltpu.make_async_copy(t_ref, t_hbm, sems.at[0]),
        pltpu.make_async_copy(drive_ref, drive_hbm, sems.at[1]),
    ]
    for copy in copies:
        copy.start()
    for copy in copies:
        copy.wait()


def cost(elements, ops, arrays):
    return pl.CostEstimate(flops=elements * ops, bytes_accessed=elements * 4 * arrays, transcendentals=0)


def call(kernel, name, inputs, outs, carried=(), limit=16, work=None, scratch=()):
    specs = [spec for spec, _ in inputs] + [vmem_spec] * len(carried)
    arrays = []
    for spec, array in inputs:
        if spec is hbm_spec:
            array = pltpu.with_memory_space_constraint(array, pltpu.HBM)
        elif spec is vmem_spec:
            array = pltpu.with_memory_space_constraint(array, pltpu.VMEM)
        arrays.append(array)
    arrays += [pltpu.with_memory_space_constraint(a, pltpu.VMEM) for a in carried]
    out_specs = [spec for spec, _ in outs] + [vmem_spec] * len(carried)
    out_shape = [shape for _, shape in outs] + [pltpu.VMEM(a.shape, a.dtype) for a in carried]
    return pl.pallas_call(
        kernel,
        in_specs=specs,
        out_specs=out_specs,
        out_shape=out_shape,
        scratch_shapes=list(scratch),
        input_output_aliases={len(inputs) + n: len(outs) + n for n in range(len(carried))},
        compiler_params=pltpu.CompilerParams(vmem_limit_bytes=limit * 2**20),
        cost_estimate=work,
        name=name,
    )(*arrays)


def exchange(x, axis, mask):
    return lax.ppermute(x, axis, [(i, i ^ mask) for i in range(lax.axis_size(axis))])


def per_device(electric_x, electric_z, magnetic_x, magnetic_y, magnetic_z, material, perm_table):
    xs, ys, zs = material.shape
    chunks = xs // rows
    cells = xs * ys * zs
    V, H = pltpu.VMEM, pltpu.HBM
    fields = (electric_x, electric_z, magnetic_x, magnetic_y, magnetic_z)
    block = (2 * chunks, 5, 2 * rows, lane)

    y_t, y_drive, y_reduced, x_t, x_drive, x_reduced, yt_edge, my_edge, xt_edge, mx_edge = call(
        forward_kernel,
        "forward",
        [(hbm_spec, a) for a in (perm_table, material) + fields],
        [
            (vmem_spec, V((ys, xs, zs), f32)),
            (vmem_spec, V((ys, xs, zs), f32)),
            (vmem_spec, V(block, f32)),
            (vmem_spec, V((xs, ys, zs), f32)),
            (vmem_spec, V((xs, ys, zs), f32)),
            (vmem_spec, V((5, ys, zs), f32)),
            (vmem_spec, V((ys, xs, lane), f32)),
            (vmem_spec, V((rows, lane), f32)),
            (vmem_spec, V((xs, 1, zs), f32)),
            (vmem_spec, V((xs, zs), f32)),
        ],
        scratch=[pltpu.SMEM(perm_table.shape, f32), V((xs, ys, zs), jnp.int32)]
        + [V((xs, ys, zs), f32)] * 5
        + [V((zs // lane, rows * ys, lane), f32)] * 4
        + [V((rows * ys, lane), f32), V((5, ys, zs), f32), V((ys, zs), f32)]
        + [pltpu.SemaphoreType.DMA, pltpu.SemaphoreType.DMA((6, chunks))],
        limit=24,
        work=cost(cells, 60, 10),
    )

    edge_z = exchange(my_edge, "gz", 1)
    count = lax.axis_size("gy")
    edge_y = lax.ppermute(mx_edge, "gy", [(i, (i + 1) % count) for i in range(count)])
    y_reduced, y_drive = pl.pallas_call(
        y_edge_kernel,
        in_specs=[vmem_spec] * 4,
        out_specs=[vmem_spec] * 2,
        out_shape=[H(block, f32), V((ys, xs, zs), f32)],
        input_output_aliases={3: 1},
        compiler_params=pltpu.CompilerParams(vmem_limit_bytes=8 * 2**20),
        cost_estimate=cost(cells // 4, 10, 3),
        name="y_edge",
    )(*(pltpu.with_memory_space_constraint(a, V) for a in (edge_z, yt_edge, y_reduced, y_drive)))
    x_t, x_drive = call(
        store_kernel,
        "store",
        [(vmem_spec, x_t), (vmem_spec, x_drive)],
        [(hbm_spec, H((xs, ys, zs), f32))] * 2,
        scratch=[pltpu.SemaphoreType.DMA((2,))],
        limit=8,
        work=cost(cells, 1, 4),
    )
    y_reduced, edge_y, x_t, x_drive = lax.optimization_barrier(
        (y_reduced, edge_y, x_t, x_drive)
    )
    y_blocks = lax.all_to_all(y_reduced, "gy", 0, 0, tiled=True)

    x_reduced, kept = call(
        x_edge_kernel,
        "x_edge",
        [(vmem_spec, a) for a in (edge_y, xt_edge, x_reduced)],
        [(vmem_spec, V((5, ys, zs), f32)), (vmem_spec, V((kept_count, ys, zs), f32))],
        limit=8,
        work=cost(cells // ys, 10, 3),
    )

    (y_ends,) = pl.pallas_call(
        y_reduced_kernel,
        in_specs=[vmem_spec],
        out_specs=[vmem_spec],
        out_shape=[H((2 * chunks, 2, 2 * rows, lane), f32)],
        compiler_params=pltpu.CompilerParams(vmem_limit_bytes=8 * 2**20),
        cost_estimate=cost(y_blocks.size // 5, 20, 7),
        name="y_reduced",
    )(y_blocks)

    own = x_reduced
    for level, mask in enumerate((1, 3, 4)):
        other = exchange(own, "gx", mask)
        kernel = functools.partial(merge_kernel if level < 2 else last_merge_kernel, level)

        def body(own_ref, other_ref, *refs, kernel=kernel):
            merged_ref, kept_ref = refs[-4:-2]
            kernel(own_ref, other_ref, None, merged_ref, kept_ref)

        own, kept, y_t, y_drive = call(
            body,
            "x_merge",
            [(vmem_spec, own), (vmem_spec, other)] + ([(any_spec, y_ends)] if level == 1 else []),
            [(vmem_spec, V((5 if level < 2 else 2, ys, zs), f32))],
            carried=(kept, y_t, y_drive),
            limit=8,
            work=cost(own.size, 10, 3),
        )
    side_other = exchange(own, "gx", 12)
    y_ends = lax.all_to_all(y_ends, "gy", 0, 0, tiled=True)

    electric_x_half, x_t, x_drive = call(
        y_back_kernel,
        "y_back",
        [(vmem_spec, a) for a in (y_t, y_drive, y_ends)] + [(hbm_spec, a) for a in (x_t, x_drive)],
        [(hbm_spec, H((xs, ys, zs), f32))] + [(vmem_spec, V((xs, ys, zs), f32))] * 2,
        scratch=[V((zs // lane, rows * ys, lane), f32), V((xs, ys, zs), f32)]
        + [pltpu.SemaphoreType.DMA((chunks,)), pltpu.SemaphoreType.DMA((2,))],
        work=cost(cells, 5, 3),
    )
    (electric_z_half,) = call(
        x_back_kernel,
        "x_back",
        [(vmem_spec, a) for a in (x_t, x_drive, kept, own, side_other)],
        [(vmem_spec, H((xs, ys, zs), f32))],
        work=cost(cells, 5, 3),
    )
    return (electric_x_half, electric_z_half)


def solution(mesh):
    field = P("gx", "gy", "gz")
    return jax.shard_map(
        per_device,
        mesh=mesh,
        in_specs=(field,) * 6 + (P(),),
        out_specs=(field, field),
        check_vma=False,
    )
```

```python
import functools

import jax
import jax.numpy as jnp
from jax import lax
from jax.experimental import pallas as pl
from jax.experimental.pallas import tpu as pltpu
from jax.sharding import PartitionSpec as P

ground_scale = 1.0 / 1600.0
drive_scale = 1.0 / 40.0
lane = 128
rows = 8
f32 = jnp.float32
vmem_spec = pl.BlockSpec(memory_space=pltpu.VMEM)
any_spec = pl.BlockSpec(memory_space=pl.ANY)
hbm_spec = pl.BlockSpec(memory_space=pltpu.HBM)


def inverse(x):
    return pltpu.reciprocal(x, approx=True)


def eliminate(state, ground, drive):
    link, left, here, left_drive, here_drive = state
    t = inverse(link + here + 1.0)
    next_link = link * t
    return (
        next_link,
        left + next_link * here,
        ground + here * t,
        left_drive + next_link * here_drive,
        drive + here_drive * t,
    ), t


def close_block(state, rim):
    link, left, here, left_drive, here_drive = state
    return (
        link,
        left,
        here,
        left_drive + link * rim,
        here_drive - (link + here + 1.0) * rim,
    )


def forward_kernel(
    table_hbm, material_hbm, ex_hbm, ez_hbm, mx_hbm, my_hbm, mz_hbm,
    yt_ref, ydrive_ref, yreduced_ref, xt_ref, xdrive_ref, xreduced_ref,
    yt_edge_ref, my_edge_ref, xt_edge_ref, mx_edge_ref,
    table_s, material_s, ex_s, ez_s, mx_s, my_s, mz_s, ground_s, yground_s, ydrive_s, xdrive_s, turn_s,
    state_s, last_my_s, table_sem, sems,
):
    xs, ys, zs = material_s.shape
    tiles = zs // lane
    chunks = xs // rows
    flat = (rows * ys, lane)
    cube = (rows, ys, lane)
    arrays = (
        (material_hbm, material_s), (my_hbm, my_s), (mz_hbm, mz_s),
        (ex_hbm, ex_s), (ez_hbm, ez_s), (mx_hbm, mx_s),
    )

    def chunk_copies(c):
        part = pl.ds(pl.multiple_of(c * rows, rows), rows)
        return [
            pltpu.make_async_copy(source.at[part], target.at[part], sems.at[a, c])
            for a, (source, target) in enumerate(arrays)
        ]

    table_copy = pltpu.make_async_copy(table_hbm, table_s, table_sem)
    table_copy.start()
    for c in range(chunks):
        for copy in chunk_copies(c):
            copy.start()
    lanes = lax.broadcasted_iota(jnp.int32, flat, 1)
    first_lane = lanes == 0
    first_y = lax.broadcasted_iota(jnp.int32, cube, 1) == 0
    edge_lanes = lax.broadcasted_iota(jnp.int32, (rows, lane), 1)
    my_edge_ref[...] = jnp.zeros_like(my_edge_ref)
    state_s[...] = jnp.zeros_like(state_s)
    last_my_s[...] = jnp.zeros_like(last_my_s)
    table_copy.wait()
    table = jnp.zeros((1, lane), f32)
    for m in range(table_s.shape[0]):
        table = jnp.where(lax.broadcasted_iota(jnp.int32, (1, lane), 1) == m, table_s[m], table)
    table = table * ground_scale

    def chunk(c, _):
        for copy in chunk_copies(c):
            copy.wait()
        part = pl.ds(pl.multiple_of(c * rows, rows), rows)
        before = jnp.zeros(flat, f32)
        for k in range(tiles):
            cut = pl.ds(k * lane, lane)
            ground = jnp.take_along_axis(
                jnp.broadcast_to(table, flat), material_s[part, :, cut].reshape(flat), axis=1, mode="promise_in_bounds"
            )
            my = my_s[part, :, cut]
            rolled = pltpu.roll(my.reshape(flat), 1, 1)
            my_step = my.reshape(flat) - jnp.where(first_lane, before, rolled)
            before = rolled
            mz = mz_s[part, :, cut]
            mz_step = (mz - jnp.where(first_y, 0.0, pltpu.roll(mz, 1, 1))).reshape(flat)
            mx = mx_s[part, :, cut]
            mx_step = (mx - jnp.where(first_y, 0.0, pltpu.roll(mx, 1, 1))).reshape(flat)
            my_up = (my - jnp.concatenate([last_my_s[:, cut][None], my[:-1]], axis=0)).reshape(flat)
            last_my_s[:, cut] = my[rows - 1]
            ground_s[k] = ground
            ydrive = ground * ex_s[part, :, cut].reshape(flat) + drive_scale * (mz_step - my_step)
            for i in range(rows):
                for h in range(0, ys, rows):
                    turned = pl.ds(h * rows + i, rows, stride=rows)
                    natural = slice(i * ys + h, i * ys + h + rows)
                    yground_s[k, turned, :] = ground[natural]
                    ydrive_s[k, turned, :] = ydrive[natural]
            xdrive_s[k] = ground * ez_s[part, :, cut].reshape(flat) + drive_scale * (my_up - mx_step)
            mx_edge_ref[part, cut] = mx_s[part, ys - 1, cut]
            if k == tiles - 1:
                turn_s[...] = my.reshape(flat)

        states = [tuple(state_s[v, :, pl.ds(k * lane, lane)] for v in range(5)) for k in range(tiles)]
        for i in range(rows):
            line = pl.ds(i * ys, ys)
            for k in range(tiles):
                cut = pl.ds(k * lane, lane)
                state, t = eliminate(states[k], ground_s[k, line, :], xdrive_s[k, line, :])
                if i == 0:
                    state = (jnp.where(c == 0, 1.0, state[0]),) + state[1:]
                states[k] = state
                xt_ref[c * rows + i, :, cut] = t
                js = state[4]
                if i == rows - 1:
                    js = jnp.where(c == chunks - 1, drive_scale * last_my_s[:, cut], js)
                xdrive_ref[c * rows + i, :, cut] = js
                xt_edge_ref[c * rows + i, :, cut] = t[0:1]
        for k in range(tiles):
            for v in range(5):
                state_s[v, :, pl.ds(k * lane, lane)] = states[k][v]

        for first in range(0, tiles, 4):
            pair = tuple(range(first, first + 4))
            states = [None] * 4
            for j in range(ys):
                pick = pl.ds(j * rows, rows)
                for n, k in enumerate(pair):
                    cut = pl.ds(k * lane, lane)
                    ground = yground_s[k, pick, :]
                    drive = ydrive_s[k, pick, :]
                    if j == 0:
                        zero = jnp.zeros_like(ground)
                        states[n] = (jnp.ones_like(ground), zero, ground, zero, drive)
                    else:
                        states[n], t = eliminate(states[n], ground, drive)
                        yt_ref[j - 1, part, cut] = t
                        if k == 0:
                            yt_edge_ref[j - 1, part, :] = t
                    if j < ys - 1:
                        ydrive_ref[j, part, cut] = states[n][4]
            for n, k in enumerate(pair):
                cut = pl.ds(k * lane, lane)
                rim = drive_scale * mz_s[part, ys - 1, cut]
                ydrive_ref[ys - 1, part, cut] = rim
                for v, value in enumerate(close_block(states[n], rim)):
                    yreduced_ref[2 * c + k // 2, v, pl.ds((k % 2) * rows, rows), :] = value
        packed = my_edge_ref[...]
        for j in range(ys):
            place = j * chunks + c
            turned = pltpu.roll(turn_s[pl.ds(j, rows, stride=ys), :], place + 1, 1)
            packed = jnp.where(edge_lanes == place, turned, packed)
        my_edge_ref[...] = packed
        return _

    lax.fori_loop(0, chunks, chunk, 0)
    rim = drive_scale * last_my_s[...]
    for v, value in enumerate(close_block(tuple(state_s[v] for v in range(5)), rim)):
        xreduced_ref[v] = value


def y_edge_kernel(edge_ref, t_ref, reduced_ref, drive_ref, reduced_out, drive_out):
    ys, xs, _ = t_ref.shape
    reduced_out[...] = reduced_ref[...]
    first_lane = lax.broadcasted_iota(jnp.int32, (rows, lane), 1) == 0
    first_lane = first_lane & (lax.axis_index("gz") == 1)
    for c in range(xs // rows):
        part = pl.ds(c * rows, rows)

        def rim(j, c=c):
            place = j * (xs // rows) + c
            turned = pltpu.roll(edge_ref[...], (lane - place) % lane, 1)
            return jnp.where(first_lane, drive_scale * turned, 0.0)

        here = rim(0)
        link = jnp.ones_like(here)
        left = jnp.zeros_like(here)
        for j in range(ys):
            if j > 0:
                t = t_ref[j - 1, part, :]
                link = link * t
                left = left + link * here
                here = rim(j) + here * t
            if j < ys - 1:
                drive_out[j, part, pl.ds(0, lane)] = drive_ref[j, part, pl.ds(0, lane)] + here
        reduced_out[2 * c, 3, pl.ds(0, rows), :] = reduced_ref[2 * c, 3, pl.ds(0, rows), :] + left
        reduced_out[2 * c, 4, pl.ds(0, rows), :] = reduced_ref[2 * c, 4, pl.ds(0, rows), :] + here


kept_count = 13


def x_edge_kernel(edge_ref, t_ref, reduced_ref, reduced_out, kept_ref):
    xs = t_ref.shape[0]
    ys = reduced_ref.shape[1]
    row = pl.ds(0, 1)
    edge = jnp.where(lax.axis_index("gy") > 0, drive_scale, 0.0) * edge_ref[...]
    here = edge[0:1]
    link = jnp.ones_like(here)
    left = jnp.zeros_like(here)
    kept_ref[11, row, :] = here
    for i in range(1, xs):
        t = t_ref[i]
        link = link * t
        left = left + link * here
        here = edge[i:i + 1] + here * t
        kept_ref[11 + i // ys, pl.ds(i % ys, 1), :] = here
    for v in range(5):
        reduced_out[v] = reduced_ref[v]
    reduced_out[3, row, :] = reduced_ref[3, row, :] + left
    reduced_out[4, row, :] = reduced_ref[4, row, :] + here


def y_reduced_kernel(blocks_ref, ends_ref):
    count = blocks_ref.shape[0]
    block = [[blocks_ref[b, v] for v in range(5)] for b in range(count)]
    here = block[0][2] + block[0][0]
    drive = block[0][4]
    kept = []
    for b in range(1, count):
        link, left, right, left_drive, right_drive = block[b]
        total = here + left
        t = inverse(total + link)
        pull = link * t
        push = drive + left_drive
        kept.append((pull, push * t))
        here = right + pull * total
        drive = right_drive + pull * push
    value = drive * inverse(here + 1.0)
    ends_ref[count - 1, 1] = value
    for b in range(count - 1, 0, -1):
        pull, push = kept[b - 1]
        value = push + pull * value
        ends_ref[b, 0] = value
        ends_ref[b - 1, 1] = value
    ends_ref[0, 0] = jnp.zeros_like(value)


def merge(low, own_ref, other_ref, kept_ref, slot):
    own = [own_ref[v] for v in range(5)]
    other = [other_ref[v] for v in range(5)]
    a = [jnp.where(low, p, q) for p, q in zip(own, other)]
    b = [jnp.where(low, q, p) for p, q in zip(own, other)]
    total = a[2] + b[1]
    t = inverse(total + a[0] + b[0])
    a_link, b_link = a[0] * t, b[0] * t
    push = a[4] + b[3]
    kept_ref[slot] = push * t
    kept_ref[slot + 1] = a_link
    kept_ref[slot + 2] = b_link
    return (
        a[0] * b_link,
        a[1] + a_link * total,
        b[2] + b_link * total,
        a[3] + a_link * push,
        b[4] + b_link * push,
    )


def is_low(level):
    return (lax.axis_index("gx") >> level) & 1 == 0


def merge_kernel(level, own_ref, other_ref, _, merged_ref, kept_ref):
    merged = merge(is_low(level), own_ref, other_ref, kept_ref, 3 * level)
    for v in range(5):
        merged_ref[v] = merged[v]


def last_merge_kernel(level, own_ref, other_ref, _, side_ref, kept_ref):
    link, left, right, left_drive, right_drive = merge(is_low(level), own_ref, other_ref, kept_ref, 3 * level)
    closed = inverse(right + link + 1.0)
    share = link * closed
    top = is_low(level + 1)
    side_ref[0] = jnp.where(top, right + link, left + share * (right + 1.0))
    side_ref[1] = jnp.where(top, right_drive, left_drive + share * right_drive)
    kept_ref[9] = closed * right_drive
    kept_ref[10] = share


def y_back_kernel(
    t_ref, drive_ref, ends_ref, xt_hbm, xdrive_hbm, out_hbm, xt_ref, xdrive_ref, turn_s, out_s, sems, load_sems
):
    loads = [
        pltpu.make_async_copy(xt_hbm, xt_ref, load_sems.at[0]),
        pltpu.make_async_copy(xdrive_hbm, xdrive_ref, load_sems.at[1]),
    ]
    for load in loads:
        load.start()
    ys, xs, zs = t_ref.shape
    copies = []
    for c in range(xs // rows):
        part = pl.ds(c * rows, rows)
        for k in range(zs // lane):
            cut = pl.ds(k * lane, lane)
            half = pl.ds((k % 2) * rows, rows)
            reach = ends_ref[2 * c + k // 2, 0, half, :]
            value = ends_ref[2 * c + k // 2, 1, half, :] + drive_ref[ys - 1, part, cut]
            parts = []
            for j in range(ys - 1):
                t = t_ref[j, part, cut]
                reach = reach * t
                parts.append((t, drive_ref[j, part, cut] * t + reach))
            turn_s[k, pl.ds(ys - 1, rows, stride=ys), :] = value
            for j in range(ys - 2, -1, -1):
                t, share = parts[j]
                value = share + t * value
                turn_s[k, pl.ds(j, rows, stride=ys), :] = value
            out_s[part, :, cut] = turn_s[k].reshape(rows, ys, lane)
        copies.append(pltpu.make_async_copy(out_s.at[part], out_hbm.at[part], sems.at[c]))
        copies[-1].start()
    for copy in copies + loads:
        copy.wait()


def x_back_kernel(t_ref, drive_ref, kept_ref, side_ref, other_ref, out_ref):
    xs, ys, zs = t_ref.shape
    top = is_low(3)
    middle = (side_ref[1] + other_ref[1]) * inverse(side_ref[0] + other_ref[0])
    before = jnp.where(top, 0.0, middle)
    here = jnp.where(top, middle, kept_ref[9] + kept_ref[10] * middle)
    for level in (2, 1, 0):
        low = is_low(level)
        middle = kept_ref[3 * level] + kept_ref[3 * level + 1] * before + kept_ref[3 * level + 2] * here
        before, here = jnp.where(low, before, middle), jnp.where(low, middle, here)
    first_y = lax.broadcasted_iota(jnp.int32, (ys, zs), 0) == 0
    reach = before
    for i in range(xs - 1):
        t = t_ref[i + 1]
        reach = reach * t
        edge = jnp.where(first_y, kept_ref[11 + i // ys, pl.ds(i % ys, 1), :], 0.0)
        out_ref[i] = (drive_ref[i] + edge) * t + reach
    value = here + drive_ref[xs - 1]
    out_ref[xs - 1] = value
    for i in range(xs - 2, -1, -1):
        value = out_ref[i] + t_ref[i + 1] * value
        out_ref[i] = value


def store_kernel(t_ref, drive_ref, t_hbm, drive_hbm, sems):
    copies = [
        pltpu.make_async_copy(t_ref, t_hbm, sems.at[0]),
        pltpu.make_async_copy(drive_ref, drive_hbm, sems.at[1]),
    ]
    for copy in copies:
        copy.start()
    for copy in copies:
        copy.wait()


def cost(elements, ops, arrays):
    return pl.CostEstimate(flops=elements * ops, bytes_accessed=elements * 4 * arrays, transcendentals=0)


def call(kernel, name, inputs, outs, carried=(), limit=16, work=None, scratch=()):
    specs = [spec for spec, _ in inputs] + [vmem_spec] * len(carried)
    arrays = []
    for spec, array in inputs:
        if spec is hbm_spec:
            array = pltpu.with_memory_space_constraint(array, pltpu.HBM)
        elif spec is vmem_spec:
            array = pltpu.with_memory_space_constraint(array, pltpu.VMEM)
        arrays.append(array)
    arrays += [pltpu.with_memory_space_constraint(a, pltpu.VMEM) for a in carried]
    out_specs = [spec for spec, _ in outs] + [vmem_spec] * len(carried)
    out_shape = [shape for _, shape in outs] + [pltpu.VMEM(a.shape, a.dtype) for a in carried]
    return pl.pallas_call(
        kernel,
        in_specs=specs,
        out_specs=out_specs,
        out_shape=out_shape,
        scratch_shapes=list(scratch),
        input_output_aliases={len(inputs) + n: len(outs) + n for n in range(len(carried))},
        compiler_params=pltpu.CompilerParams(vmem_limit_bytes=limit * 2**20),
        cost_estimate=work,
        name=name,
    )(*arrays)


def exchange(x, axis, mask):
    return lax.ppermute(x, axis, [(i, i ^ mask) for i in range(lax.axis_size(axis))])


def per_device(electric_x, electric_z, magnetic_x, magnetic_y, magnetic_z, material, perm_table):
    xs, ys, zs = material.shape
    chunks = xs // rows
    cells = xs * ys * zs
    V, H = pltpu.VMEM, pltpu.HBM
    fields = (electric_x, electric_z, magnetic_x, magnetic_y, magnetic_z)
    block = (2 * chunks, 5, 2 * rows, lane)

    y_t, y_drive, y_reduced, x_t, x_drive, x_reduced, yt_edge, my_edge, xt_edge, mx_edge = call(
        forward_kernel,
        "forward",
        [(hbm_spec, a) for a in (perm_table, material) + fields],
        [
            (vmem_spec, V((ys, xs, zs), f32)),
            (vmem_spec, V((ys, xs, zs), f32)),
            (vmem_spec, V(block, f32)),
            (vmem_spec, V((xs, ys, zs), f32)),
            (vmem_spec, V((xs, ys, zs), f32)),
            (vmem_spec, V((5, ys, zs), f32)),
            (vmem_spec, V((ys, xs, lane), f32)),
            (vmem_spec, V((rows, lane), f32)),
            (vmem_spec, V((xs, 1, zs), f32)),
            (vmem_spec, V((xs, zs), f32)),
        ],
        scratch=[pltpu.SMEM(perm_table.shape, f32), V((xs, ys, zs), jnp.int32)]
        + [V((xs, ys, zs), f32)] * 5
        + [V((zs // lane, rows * ys, lane), f32)] * 4
        + [V((rows * ys, lane), f32), V((5, ys, zs), f32), V((ys, zs), f32)]
        + [pltpu.SemaphoreType.DMA, pltpu.SemaphoreType.DMA((6, chunks))],
        limit=24,
        work=cost(cells, 60, 10),
    )

    edge_z = exchange(my_edge, "gz", 1)
    count = lax.axis_size("gy")
    edge_y = lax.ppermute(mx_edge, "gy", [(i, (i + 1) % count) for i in range(count)])
    y_reduced, y_drive = pl.pallas_call(
        y_edge_kernel,
        in_specs=[vmem_spec] * 4,
        out_specs=[vmem_spec] * 2,
        out_shape=[H(block, f32), V((ys, xs, zs), f32)],
        input_output_aliases={3: 1},
        compiler_params=pltpu.CompilerParams(vmem_limit_bytes=8 * 2**20),
        cost_estimate=cost(cells // 4, 10, 3),
        name="y_edge",
    )(*(pltpu.with_memory_space_constraint(a, V) for a in (edge_z, yt_edge, y_reduced, y_drive)))
    x_t, x_drive = call(
        store_kernel,
        "store",
        [(vmem_spec, x_t), (vmem_spec, x_drive)],
        [(hbm_spec, H((xs, ys, zs), f32))] * 2,
        scratch=[pltpu.SemaphoreType.DMA((2,))],
        limit=8,
        work=cost(cells, 1, 4),
    )
    y_reduced, edge_y, x_t, x_drive = lax.optimization_barrier(
        (y_reduced, edge_y, x_t, x_drive)
    )
    y_blocks = lax.all_to_all(y_reduced, "gy", 0, 0, tiled=True)

    x_reduced, kept = call(
        x_edge_kernel,
        "x_edge",
        [(vmem_spec, a) for a in (edge_y, xt_edge, x_reduced)],
        [(vmem_spec, V((5, ys, zs), f32)), (vmem_spec, V((kept_count, ys, zs), f32))],
        limit=8,
        work=cost(cells // ys, 10, 3),
    )

    (y_ends,) = pl.pallas_call(
        y_reduced_kernel,
        in_specs=[vmem_spec],
        out_specs=[vmem_spec],
        out_shape=[H((2 * chunks, 2, 2 * rows, lane), f32)],
        compiler_params=pltpu.CompilerParams(vmem_limit_bytes=8 * 2**20),
        cost_estimate=cost(y_blocks.size // 5, 20, 7),
        name="y_reduced",
    )(y_blocks)

    own = x_reduced
    for level, mask in enumerate((1, 3, 4)):
        other = exchange(own, "gx", mask)
        kernel = functools.partial(merge_kernel if level < 2 else last_merge_kernel, level)

        def body(own_ref, other_ref, *refs, kernel=kernel):
            merged_ref, kept_ref = refs[-4:-2]
            kernel(own_ref, other_ref, None, merged_ref, kept_ref)

        own, kept, y_t, y_drive = call(
            body,
            "x_merge",
            [(vmem_spec, own), (vmem_spec, other)] + ([(any_spec, y_ends)] if level == 1 else []),
            [(vmem_spec, V((5 if level < 2 else 2, ys, zs), f32))],
            carried=(kept, y_t, y_drive),
            limit=8,
            work=cost(own.size, 10, 3),
        )
    side_other = exchange(own, "gx", 12)
    y_ends = lax.all_to_all(y_ends, "gy", 0, 0, tiled=True)

    electric_x_half, x_t, x_drive = call(
        y_back_kernel,
        "y_back",
        [(vmem_spec, a) for a in (y_t, y_drive, y_ends)] + [(hbm_spec, a) for a in (x_t, x_drive)],
        [(hbm_spec, H((xs, ys, zs), f32))] + [(vmem_spec, V((xs, ys, zs), f32))] * 2,
        scratch=[V((zs // lane, rows * ys, lane), f32), V((xs, ys, zs), f32)]
        + [pltpu.SemaphoreType.DMA((chunks,)), pltpu.SemaphoreType.DMA((2,))],
        work=cost(cells, 5, 3),
    )
    (electric_z_half,) = call(
        x_back_kernel,
        "x_back",
        [(vmem_spec, a) for a in (x_t, x_drive, kept, own, side_other)],
        [(vmem_spec, H((xs, ys, zs), f32))],
        work=cost(cells, 5, 3),
    )
    return (electric_x_half, electric_z_half)


def solution(mesh):
    field = P("gx", "gy", "gz")
    return jax.shard_map(
        per_device,
        mesh=mesh,
        in_specs=(field,) * 6 + (P(),),
        out_specs=(field, field),
        check_vma=False,
    )
```

```python
import functools

import jax
import jax.numpy as jnp
from jax import lax
from jax.experimental import pallas as pl
from jax.experimental.pallas import tpu as pltpu
from jax.sharding import PartitionSpec as P

ground_scale = 1.0 / 1600.0
drive_scale = 1.0 / 40.0
lane = 128
rows = 8
f32 = jnp.float32
vmem_spec = pl.BlockSpec(memory_space=pltpu.VMEM)
free_spec = pl.BlockSpec(memory_space=pltpu.VMEM)
any_spec = pl.BlockSpec(memory_space=pl.ANY)
hbm_spec = pl.BlockSpec(memory_space=pltpu.HBM)


def inverse(x):
    return pltpu.reciprocal(x, approx=True)


def eliminate(state, ground, drive):
    link, left, here, left_drive, here_drive = state
    t = inverse(link + here + 1.0)
    next_link = link * t
    return (
        next_link,
        left + next_link * here,
        ground + here * t,
        left_drive + next_link * here_drive,
        drive + here_drive * t,
    ), t


def close_block(state, rim):
    link, left, here, left_drive, here_drive = state
    return (
        link,
        left,
        here,
        left_drive + link * rim,
        here_drive - (link + here + 1.0) * rim,
    )


def forward_kernel(
    table_hbm, material_hbm, ex_hbm, ez_hbm, mx_hbm, my_hbm, mz_hbm,
    yt_ref, ydrive_ref, yreduced_ref, xt_ref, xdrive_ref, xreduced_ref,
    yt_edge_ref, my_edge_ref, xt_edge_ref, mx_edge_ref,
    table_s, material_s, ex_s, ez_s, mx_s, my_s, mz_s, ground_s, yground_s, ydrive_s, xdrive_s, turn_s,
    state_s, last_my_s, table_sem, sems,
):
    xs, ys, zs = material_s.shape
    tiles = zs // lane
    chunks = xs // rows
    flat = (rows * ys, lane)
    cube = (rows, ys, lane)
    arrays = (
        (material_hbm, material_s), (my_hbm, my_s), (mz_hbm, mz_s),
        (ex_hbm, ex_s), (ez_hbm, ez_s), (mx_hbm, mx_s),
    )

    def chunk_copies(c):
        part = pl.ds(pl.multiple_of(c * rows, rows), rows)
        return [
            pltpu.make_async_copy(source.at[part], target.at[part], sems.at[a, c])
            for a, (source, target) in enumerate(arrays)
        ]

    table_copy = pltpu.make_async_copy(table_hbm, table_s, table_sem)
    table_copy.start()
    for c in range(chunks):
        for copy in chunk_copies(c):
            copy.start()
    lanes = lax.broadcasted_iota(jnp.int32, flat, 1)
    first_lane = lanes == 0
    first_y = lax.broadcasted_iota(jnp.int32, cube, 1) == 0
    edge_lanes = lax.broadcasted_iota(jnp.int32, (rows, lane), 1)
    my_edge_ref[...] = jnp.zeros_like(my_edge_ref)
    state_s[...] = jnp.zeros_like(state_s)
    last_my_s[...] = jnp.zeros_like(last_my_s)
    table_copy.wait()
    table = jnp.zeros((1, lane), f32)
    for m in range(table_s.shape[0]):
        table = jnp.where(lax.broadcasted_iota(jnp.int32, (1, lane), 1) == m, table_s[m], table)
    table = table * ground_scale

    def chunk(c, _):
        for copy in chunk_copies(c):
            copy.wait()
        part = pl.ds(pl.multiple_of(c * rows, rows), rows)
        before = jnp.zeros(flat, f32)
        for k in range(tiles):
            cut = pl.ds(k * lane, lane)
            ground = jnp.take_along_axis(
                jnp.broadcast_to(table, flat), material_s[part, :, cut].reshape(flat), axis=1, mode="promise_in_bounds"
            )
            my = my_s[part, :, cut]
            rolled = pltpu.roll(my.reshape(flat), 1, 1)
            my_step = my.reshape(flat) - jnp.where(first_lane, before, rolled)
            before = rolled
            mz = mz_s[part, :, cut]
            mz_step = (mz - jnp.where(first_y, 0.0, pltpu.roll(mz, 1, 1))).reshape(flat)
            mx = mx_s[part, :, cut]
            mx_step = (mx - jnp.where(first_y, 0.0, pltpu.roll(mx, 1, 1))).reshape(flat)
            my_up = (my - jnp.concatenate([last_my_s[:, cut][None], my[:-1]], axis=0)).reshape(flat)
            last_my_s[:, cut] = my[rows - 1]
            ground_s[k] = ground
            ydrive = ground * ex_s[part, :, cut].reshape(flat) + drive_scale * (mz_step - my_step)
            for i in range(rows):
                for h in range(0, ys, rows):
                    turned = pl.ds(h * rows + i, rows, stride=rows)
                    natural = slice(i * ys + h, i * ys + h + rows)
                    yground_s[k, turned, :] = ground[natural]
                    ydrive_s[k, turned, :] = ydrive[natural]
            xdrive_s[k] = ground * ez_s[part, :, cut].reshape(flat) + drive_scale * (my_up - mx_step)
            mx_edge_ref[part, cut] = mx_s[part, ys - 1, cut]
            if k == tiles - 1:
                turn_s[...] = my.reshape(flat)

        states = [tuple(state_s[v, :, pl.ds(k * lane, lane)] for v in range(5)) for k in range(tiles)]
        for i in range(rows):
            line = pl.ds(i * ys, ys)
            for k in range(tiles):
                cut = pl.ds(k * lane, lane)
                state, t = eliminate(states[k], ground_s[k, line, :], xdrive_s[k, line, :])
                if i == 0:
                    state = (jnp.where(c == 0, 1.0, state[0]),) + state[1:]
                states[k] = state
                xt_ref[c * rows + i, :, cut] = t
                js = state[4]
                if i == rows - 1:
                    js = jnp.where(c == chunks - 1, drive_scale * last_my_s[:, cut], js)
                xdrive_ref[c * rows + i, :, cut] = js
                xt_edge_ref[c * rows + i, :, cut] = t[0:1]
        for k in range(tiles):
            for v in range(5):
                state_s[v, :, pl.ds(k * lane, lane)] = states[k][v]

        for first in range(0, tiles, 4):
            pair = tuple(range(first, first + 4))
            states = [None] * 4
            for j in range(ys):
                pick = pl.ds(j * rows, rows)
                for n, k in enumerate(pair):
                    cut = pl.ds(k * lane, lane)
                    ground = yground_s[k, pick, :]
                    drive = ydrive_s[k, pick, :]
                    if j == 0:
                        zero = jnp.zeros_like(ground)
                        states[n] = (jnp.ones_like(ground), zero, ground, zero, drive)
                    else:
                        states[n], t = eliminate(states[n], ground, drive)
                        yt_ref[j - 1, part, cut] = t
                        if k == 0:
                            yt_edge_ref[j - 1, part, :] = t
                    if j < ys - 1:
                        ydrive_ref[j, part, cut] = states[n][4]
            for n, k in enumerate(pair):
                cut = pl.ds(k * lane, lane)
                rim = drive_scale * mz_s[part, ys - 1, cut]
                ydrive_ref[ys - 1, part, cut] = rim
                for v, value in enumerate(close_block(states[n], rim)):
                    yreduced_ref[2 * c + k // 2, v, pl.ds((k % 2) * rows, rows), :] = value
        packed = my_edge_ref[...]
        for j in range(ys):
            place = j * chunks + c
            turned = pltpu.roll(turn_s[pl.ds(j, rows, stride=ys), :], place + 1, 1)
            packed = jnp.where(edge_lanes == place, turned, packed)
        my_edge_ref[...] = packed
        return _

    lax.fori_loop(0, chunks, chunk, 0)
    rim = drive_scale * last_my_s[...]
    for v, value in enumerate(close_block(tuple(state_s[v] for v in range(5)), rim)):
        xreduced_ref[v] = value


def y_edge_kernel(edge_ref, t_ref, reduced_ref, drive_ref, reduced_out, drive_out):
    ys, xs, _ = t_ref.shape
    reduced_out[...] = reduced_ref[...]
    first_lane = lax.broadcasted_iota(jnp.int32, (rows, lane), 1) == 0
    first_lane = first_lane & (lax.axis_index("gz") == 1)
    for c in range(xs // rows):
        part = pl.ds(c * rows, rows)

        def rim(j, c=c):
            place = j * (xs // rows) + c
            turned = pltpu.roll(edge_ref[...], (lane - place) % lane, 1)
            return jnp.where(first_lane, drive_scale * turned, 0.0)

        here = rim(0)
        link = jnp.ones_like(here)
        left = jnp.zeros_like(here)
        for j in range(ys):
            if j > 0:
                t = t_ref[j - 1, part, :]
                link = link * t
                left = left + link * here
                here = rim(j) + here * t
            if j < ys - 1:
                drive_out[j, part, pl.ds(0, lane)] = drive_ref[j, part, pl.ds(0, lane)] + here
        reduced_out[2 * c, 3, pl.ds(0, rows), :] = reduced_ref[2 * c, 3, pl.ds(0, rows), :] + left
        reduced_out[2 * c, 4, pl.ds(0, rows), :] = reduced_ref[2 * c, 4, pl.ds(0, rows), :] + here


kept_count = 13


def x_edge_kernel(edge_ref, t_ref, reduced_ref, reduced_out, kept_ref):
    xs = t_ref.shape[0]
    ys = reduced_ref.shape[1]
    row = pl.ds(0, 1)
    edge = jnp.where(lax.axis_index("gy") > 0, drive_scale, 0.0) * edge_ref[...]
    here = edge[0:1]
    link = jnp.ones_like(here)
    left = jnp.zeros_like(here)
    kept_ref[11, row, :] = here
    for i in range(1, xs):
        t = t_ref[i]
        link = link * t
        left = left + link * here
        here = edge[i:i + 1] + here * t
        kept_ref[11 + i // ys, pl.ds(i % ys, 1), :] = here
    for v in range(5):
        reduced_out[v] = reduced_ref[v]
    reduced_out[3, row, :] = reduced_ref[3, row, :] + left
    reduced_out[4, row, :] = reduced_ref[4, row, :] + here


def y_reduced_kernel(blocks_ref, ends_ref):
    count = blocks_ref.shape[0]
    block = [[blocks_ref[b, v] for v in range(5)] for b in range(count)]
    here = block[0][2] + block[0][0]
    drive = block[0][4]
    kept = []
    for b in range(1, count):
        link, left, right, left_drive, right_drive = block[b]
        total = here + left
        t = inverse(total + link)
        pull = link * t
        push = drive + left_drive
        kept.append((pull, push * t))
        here = right + pull * total
        drive = right_drive + pull * push
    value = drive * inverse(here + 1.0)
    ends_ref[count - 1, 1] = value
    for b in range(count - 1, 0, -1):
        pull, push = kept[b - 1]
        value = push + pull * value
        ends_ref[b, 0] = value
        ends_ref[b - 1, 1] = value
    ends_ref[0, 0] = jnp.zeros_like(value)


def merge(low, own_ref, other_ref, kept_ref, slot):
    own = [own_ref[v] for v in range(5)]
    other = [other_ref[v] for v in range(5)]
    a = [jnp.where(low, p, q) for p, q in zip(own, other)]
    b = [jnp.where(low, q, p) for p, q in zip(own, other)]
    total = a[2] + b[1]
    t = inverse(total + a[0] + b[0])
    a_link, b_link = a[0] * t, b[0] * t
    push = a[4] + b[3]
    kept_ref[slot] = push * t
    kept_ref[slot + 1] = a_link
    kept_ref[slot + 2] = b_link
    return (
        a[0] * b_link,
        a[1] + a_link * total,
        b[2] + b_link * total,
        a[3] + a_link * push,
        b[4] + b_link * push,
    )


def is_low(level):
    return (lax.axis_index("gx") >> level) & 1 == 0


def merge_kernel(level, own_ref, other_ref, _, merged_ref, kept_ref):
    merged = merge(is_low(level), own_ref, other_ref, kept_ref, 3 * level)
    for v in range(5):
        merged_ref[v] = merged[v]


def last_merge_kernel(level, own_ref, other_ref, _, side_ref, kept_ref):
    link, left, right, left_drive, right_drive = merge(is_low(level), own_ref, other_ref, kept_ref, 3 * level)
    closed = inverse(right + link + 1.0)
    share = link * closed
    top = is_low(level + 1)
    side_ref[0] = jnp.where(top, right + link, left + share * (right + 1.0))
    side_ref[1] = jnp.where(top, right_drive, left_drive + share * right_drive)
    kept_ref[9] = closed * right_drive
    kept_ref[10] = share


def y_back_kernel(
    t_ref, drive_ref, ends_ref, xt_hbm, out_hbm, xt_ref, turn_s, out_s, sems, load_sem
):
    loads = [pltpu.make_async_copy(xt_hbm, xt_ref, load_sem)]
    for load in loads:
        load.start()
    ys, xs, zs = t_ref.shape
    copies = []
    for c in range(xs // rows):
        part = pl.ds(c * rows, rows)
        for k in range(zs // lane):
            cut = pl.ds(k * lane, lane)
            half = pl.ds((k % 2) * rows, rows)
            reach = ends_ref[2 * c + k // 2, 0, half, :]
            value = ends_ref[2 * c + k // 2, 1, half, :] + drive_ref[ys - 1, part, cut]
            parts = []
            for j in range(ys - 1):
                t = t_ref[j, part, cut]
                reach = reach * t
                parts.append((t, drive_ref[j, part, cut] * t + reach))
            turn_s[k, pl.ds(ys - 1, rows, stride=ys), :] = value
            for j in range(ys - 2, -1, -1):
                t, share = parts[j]
                value = share + t * value
                turn_s[k, pl.ds(j, rows, stride=ys), :] = value
            out_s[part, :, cut] = turn_s[k].reshape(rows, ys, lane)
        copies.append(pltpu.make_async_copy(out_s.at[part], out_hbm.at[part], sems.at[c]))
        copies[-1].start()
    for copy in copies + loads:
        copy.wait()


def x_back_kernel(t_ref, drive_ref, kept_ref, side_ref, other_ref, out_ref):
    xs, ys, zs = t_ref.shape
    top = is_low(3)
    middle = (side_ref[1] + other_ref[1]) * inverse(side_ref[0] + other_ref[0])
    before = jnp.where(top, 0.0, middle)
    here = jnp.where(top, middle, kept_ref[9] + kept_ref[10] * middle)
    for level in (2, 1, 0):
        low = is_low(level)
        middle = kept_ref[3 * level] + kept_ref[3 * level + 1] * before + kept_ref[3 * level + 2] * here
        before, here = jnp.where(low, before, middle), jnp.where(low, middle, here)
    first_y = lax.broadcasted_iota(jnp.int32, (ys, zs), 0) == 0
    reach = before
    for i in range(xs - 1):
        t = t_ref[i + 1]
        reach = reach * t
        edge = jnp.where(first_y, kept_ref[11 + i // ys, pl.ds(i % ys, 1), :], 0.0)
        out_ref[i] = (drive_ref[i] + edge) * t + reach
    value = here + drive_ref[xs - 1]
    out_ref[xs - 1] = value
    for i in range(xs - 2, -1, -1):
        value = out_ref[i] + t_ref[i + 1] * value
        out_ref[i] = value


def store_kernel(t_ref, drive_ref, t_hbm, drive_hbm, sems):
    copies = [
        pltpu.make_async_copy(t_ref, t_hbm, sems.at[0]),
        pltpu.make_async_copy(drive_ref, drive_hbm, sems.at[1]),
    ]
    for copy in copies:
        copy.start()
    for copy in copies:
        copy.wait()


def cost(elements, ops, arrays):
    return pl.CostEstimate(flops=elements * ops, bytes_accessed=elements * 4 * arrays, transcendentals=0)


def call(kernel, name, inputs, outs, carried=(), limit=16, work=None, scratch=()):
    specs = [spec for spec, _ in inputs] + [vmem_spec] * len(carried)
    arrays = []
    for spec, array in inputs:
        if spec is hbm_spec:
            array = pltpu.with_memory_space_constraint(array, pltpu.HBM)
        elif spec is vmem_spec:
            array = pltpu.with_memory_space_constraint(array, pltpu.VMEM)
        arrays.append(array)
    arrays += [pltpu.with_memory_space_constraint(a, pltpu.VMEM) for a in carried]
    out_specs = [spec for spec, _ in outs] + [vmem_spec] * len(carried)
    out_shape = [shape for _, shape in outs] + [pltpu.VMEM(a.shape, a.dtype) for a in carried]
    return pl.pallas_call(
        kernel,
        in_specs=specs,
        out_specs=out_specs,
        out_shape=out_shape,
        scratch_shapes=list(scratch),
        input_output_aliases={len(inputs) + n: len(outs) + n for n in range(len(carried))},
        compiler_params=pltpu.CompilerParams(vmem_limit_bytes=limit * 2**20),
        cost_estimate=work,
        name=name,
    )(*arrays)


def exchange(x, axis, mask):
    return lax.ppermute(x, axis, [(i, i ^ mask) for i in range(lax.axis_size(axis))])


def per_device(electric_x, electric_z, magnetic_x, magnetic_y, magnetic_z, material, perm_table):
    xs, ys, zs = material.shape
    chunks = xs // rows
    cells = xs * ys * zs
    V, H = pltpu.VMEM, pltpu.HBM
    fields = (electric_x, electric_z, magnetic_x, magnetic_y, magnetic_z)
    block = (2 * chunks, 5, 2 * rows, lane)

    y_t, y_drive, y_reduced, x_t, x_drive, x_reduced, yt_edge, my_edge, xt_edge, mx_edge = call(
        forward_kernel,
        "forward",
        [(hbm_spec, a) for a in (perm_table, material) + fields],
        [
            (vmem_spec, V((ys, xs, zs), f32)),
            (vmem_spec, V((ys, xs, zs), f32)),
            (vmem_spec, V(block, f32)),
            (vmem_spec, V((xs, ys, zs), f32)),
            (vmem_spec, V((xs, ys, zs), f32)),
            (vmem_spec, V((5, ys, zs), f32)),
            (vmem_spec, V((ys, xs, lane), f32)),
            (vmem_spec, V((rows, lane), f32)),
            (vmem_spec, V((xs, 1, zs), f32)),
            (vmem_spec, V((xs, zs), f32)),
        ],
        scratch=[pltpu.SMEM(perm_table.shape, f32), V((xs, ys, zs), jnp.int32)]
        + [V((xs, ys, zs), f32)] * 5
        + [V((zs // lane, rows * ys, lane), f32)] * 4
        + [V((rows * ys, lane), f32), V((5, ys, zs), f32), V((ys, zs), f32)]
        + [pltpu.SemaphoreType.DMA, pltpu.SemaphoreType.DMA((6, chunks))],
        limit=24,
        work=cost(cells, 60, 10),
    )

    edge_z = exchange(my_edge, "gz", 1)
    count = lax.axis_size("gy")
    edge_y = lax.ppermute(mx_edge, "gy", [(i, (i + 1) % count) for i in range(count)])
    y_reduced, y_drive = pl.pallas_call(
        y_edge_kernel,
        in_specs=[vmem_spec] * 4,
        out_specs=[vmem_spec] * 2,
        out_shape=[H(block, f32), V((ys, xs, zs), f32)],
        input_output_aliases={3: 1},
        compiler_params=pltpu.CompilerParams(vmem_limit_bytes=8 * 2**20),
        cost_estimate=cost(cells // 4, 10, 3),
        name="y_edge",
    )(*(pltpu.with_memory_space_constraint(a, V) for a in (edge_z, yt_edge, y_reduced, y_drive)))
    x_t, x_drive = call(
        store_kernel,
        "store",
        [(vmem_spec, x_t), (vmem_spec, x_drive)],
        [(hbm_spec, H((xs, ys, zs), f32))] * 2,
        scratch=[pltpu.SemaphoreType.DMA((2,))],
        limit=8,
        work=cost(cells, 1, 4),
    )
    y_reduced, edge_y, x_t, x_drive = lax.optimization_barrier(
        (y_reduced, edge_y, x_t, x_drive)
    )
    y_blocks = lax.all_to_all(y_reduced, "gy", 0, 0, tiled=True)

    x_reduced, kept = call(
        x_edge_kernel,
        "x_edge",
        [(vmem_spec, a) for a in (edge_y, xt_edge, x_reduced)],
        [(vmem_spec, V((5, ys, zs), f32)), (vmem_spec, V((kept_count, ys, zs), f32))],
        limit=8,
        work=cost(cells // ys, 10, 3),
    )

    (y_ends,) = pl.pallas_call(
        y_reduced_kernel,
        in_specs=[vmem_spec],
        out_specs=[vmem_spec],
        out_shape=[H((2 * chunks, 2, 2 * rows, lane), f32)],
        compiler_params=pltpu.CompilerParams(vmem_limit_bytes=8 * 2**20),
        cost_estimate=cost(y_blocks.size // 5, 20, 7),
        name="y_reduced",
    )(y_blocks)

    own = x_reduced
    for level, mask in enumerate((1, 3, 4)):
        other = exchange(own, "gx", mask)
        kernel = functools.partial(merge_kernel if level < 2 else last_merge_kernel, level)

        def body(own_ref, other_ref, *refs, kernel=kernel):
            merged_ref, kept_ref = refs[-4:-2]
            kernel(own_ref, other_ref, None, merged_ref, kept_ref)

        own, kept, y_t, y_drive = call(
            body,
            "x_merge",
            [(vmem_spec, own), (vmem_spec, other)] + ([(any_spec, y_ends)] if level == 1 else []),
            [(vmem_spec, V((5 if level < 2 else 2, ys, zs), f32))],
            carried=(kept, y_t, y_drive),
            limit=8,
            work=cost(own.size, 10, 3),
        )
    side_other = exchange(own, "gx", 12)
    y_ends = lax.all_to_all(y_ends, "gy", 0, 0, tiled=True)

    electric_x_half, x_t = call(
        y_back_kernel,
        "y_back",
        [(vmem_spec, a) for a in (y_t, y_drive, y_ends)] + [(hbm_spec, x_t)],
        [(hbm_spec, H((xs, ys, zs), f32)), (vmem_spec, V((xs, ys, zs), f32))],
        scratch=[V((zs // lane, rows * ys, lane), f32), V((xs, ys, zs), f32)]
        + [pltpu.SemaphoreType.DMA((chunks,)), pltpu.SemaphoreType.DMA],
        work=cost(cells, 5, 3),
    )
    (electric_z_half,) = call(
        x_back_kernel,
        "x_back",
        [(vmem_spec, x_t), (free_spec, x_drive)] + [(vmem_spec, a) for a in (kept, own, side_other)],
        [(vmem_spec, H((xs, ys, zs), f32))],
        work=cost(cells, 5, 3),
    )
    return (electric_x_half, electric_z_half)


def solution(mesh):
    field = P("gx", "gy", "gz")
    return jax.shard_map(
        per_device,
        mesh=mesh,
        in_specs=(field,) * 6 + (P(),),
        out_specs=(field, field),
        check_vma=False,
    )
```
